32 devices in a mesh: rep: 2 (over y), seq: 8 (over z, x), head: 2 (over core).
Axes of the slice: x: 2, y: 2, z: 4, core: 2. Of those that a mesh axis runs over, the one named last changes fastest.
Arguments:
- x_in: bfloat16 [1024, 1024], P(('rep', 'seq'), 'head'), parts along dimension 0, may hold values from -6 to 6
- b_in: bfloat16 [1024, 2048], P(('rep', 'seq'), 'head'), parts along dimension 0, may hold values from -6 to 6
- c_in: bfloat16 [1024, 2048], P(('rep', 'seq'), 'head'), parts along dimension 0, may hold values from -6 to 6
- z_in: bfloat16 [1024, 1024], P(('rep', 'seq'), 'head'), parts along dimension 0, may hold values from -6 to 6
- dt_raw: bfloat16 [1024, 16], P(('rep', 'seq'), 'head'), parts along dimension 0, may hold values from -3 to 6
- dt_bias: float32 [16], P('head'), may hold values from -4 to -3
- a_log: float32 [16], P('head')
- d_skip: float32 [16], P('head'), may hold values from 0.5 to 1.5
- conv_x: bfloat16 [4, 1024], P(None, 'head'), may hold values from -3 to 3
- conv_b: bfloat16 [4, 2048], P(None, 'head'), may hold values from -3 to 3
- conv_c: bfloat16 [4, 2048], P(None, 'head'), may hold values from -3 to 3
- norm_gain: float32 [1024], P('head'), may hold values from 0.5 to 1.5
Outputs:
- mixed: bfloat16 [1024, 1024], P(('rep', 'seq'), 'head'), parts along dimension 0
The draws below stay inside these ranges and needn't reach their ends.
There are 2 independent parts, one for each index of `rep`. The reference program is written for one: setup_inputs(seed, part) draws one part's arguments, and reference() takes and returns one part's arrays. A program takes and returns all parts, laid end to end along the dimension named above; an argument that names none is the same for every part. Nothing has to cross between parts.
All inputs are finite; a program needn't handle non-finite values.
Results may differ from the reference program's by a relative error of at most 0.0051.
Values may be sent and summed in bfloat16 or wider, within the bound.
A program may use at most 64 MiB of HBM per device.

```python
import jax
import jax.numpy as jnp
from jax import lax

HEAD_DIM = 64
STATE = 256
GROUPS = 8
CONV = 4
BLOCK = 256
HEADS = 16
TOKENS = 512


def draw_dt_raw(key, part):
    first_key, second_key = jax.random.split(jax.random.fold_in(key, 11))
    base = jnp.clip(0.5 * jax.random.normal(first_key, (TOKENS, HEADS), jnp.float32), -3.0, 3.0)
    spots = jax.random.randint(second_key, (8,), 0, TOKENS)
    positions = jnp.arange(TOKENS)[:, None]
    struck = jnp.any(positions == spots[None, :], axis=1)
    return (base + jnp.where(struck, 3.0, 0.0)[:, None]).astype(jnp.bfloat16)


def draw_a_log(key, part):
    first_key, second_key, third_key = jax.random.split(jax.random.fold_in(key, 23), 3)
    slow = jax.random.randint(first_key, (HEADS,), 0, 2) == 0
    slow_rate = jax.random.uniform(second_key, (HEADS,), jnp.float32, 0.3, 1.0) / (0.03 * TOKENS)
    fast_rate = jax.random.uniform(third_key, (HEADS,), jnp.float32, 0.5, 1.5)
    return jnp.log(jnp.where(slow, slow_rate, fast_rate))


def shard_levels(own_key, shape, pieces, smallest, high):
    loudness, own = 1.0, jax.random.fold_in(own_key, 6)
    for position, shards_of in pieces:
        heights = jnp.exp(jax.random.uniform(jax.random.fold_in(own, position), (shards_of,), jnp.float32, smallest / len(pieces), high / len(pieces)))
        loudness = loudness * jnp.repeat(heights, shape[position] // shards_of).reshape([-1 if axis == position else 1 for axis in range(len(shape))])
    return loudness


def gaussian(rng, dims, deviation, most, cuts=(), kind=jnp.bfloat16):
    level = shard_levels(rng, dims, cuts, -0.22, 0.18) if cuts else 1.0
    drawn = jax.random.normal(rng, dims, jnp.float32) * deviation * level
    return jnp.minimum(jnp.maximum(drawn, -most), most).astype(kind)


def setup_inputs(seed: int = 0, part: int = 0) -> dict:
    streams_of = jax.random.split(jax.random.key(seed), 13)
    part_splits = jax.random.split(jax.random.fold_in(streams_of[12], part), 13)
    x_in = gaussian(part_splits[0], (TOKENS, HEADS * HEAD_DIM), 1.0, 6.0, ((0, 8), (1, 2)))
    b_in = gaussian(part_splits[1], (TOKENS, GROUPS * STATE), 1.0, 6.0, ((0, 8), (1, 2)))
    c_in = gaussian(part_splits[2], (TOKENS, GROUPS * STATE), 1.0, 6.0, ((0, 8), (1, 2)))
    z_in = gaussian(part_splits[3], (TOKENS, HEADS * HEAD_DIM), 1.0, 6.0, ((0, 8), (1, 2)))
    dt_raw = draw_dt_raw(jax.random.fold_in(jax.random.fold_in(streams_of[12], part), 71), part)
    dt_bias = jnp.clip(-4.0 + 1.0 * jax.random.uniform(streams_of[5], (HEADS,), jnp.float32) ** shard_levels(streams_of[5], (HEADS,), ((0, 2),), -0.2, 0.2), -4.0, -3.0)
    a_log = draw_a_log(jax.random.fold_in(streams_of[12], 71), part)
    d_skip = jnp.clip(0.5 + 1.0 * jax.random.uniform(streams_of[7], (HEADS,), jnp.float32) ** shard_levels(streams_of[7], (HEADS,), ((0, 2),), -0.2, 0.2), 0.5, 1.5)
    conv_x = gaussian(streams_of[8], (CONV, HEADS * HEAD_DIM), CONV ** -0.5, 3.0, ((1, 2),))
    conv_b = gaussian(streams_of[9], (CONV, GROUPS * STATE), CONV ** -0.5, 3.0, ((1, 2),))
    conv_c = gaussian(streams_of[10], (CONV, GROUPS * STATE), CONV ** -0.5, 3.0, ((1, 2),))
    norm_gain = jnp.clip(1.0 + 0.1 * jax.random.normal(streams_of[11], (HEADS * HEAD_DIM,), jnp.float32), 0.5, 1.5)
    return {"x_in": x_in, "b_in": b_in, "c_in": c_in, "z_in": z_in, "dt_raw": dt_raw, "dt_bias": dt_bias, "a_log": a_log, "d_skip": d_skip, "conv_x": conv_x, "conv_b": conv_b, "conv_c": conv_c, "norm_gain": norm_gain}


def causal_conv(signal, kernel):
    taps_total = kernel.shape[0]
    length = signal.shape[0]
    padded = jnp.pad(signal, ((taps_total - 1, 0), (0, 0)))
    summed = jnp.zeros(signal.shape, jnp.float32)
    for offset in range(taps_total):
        summed = summed + kernel[offset].astype(jnp.float32) * padded[offset:offset + length].astype(jnp.float32)
    return jax.nn.silu(summed).astype(jnp.bfloat16)

def blockwise_scan(x_head, b_head, c_head, rates, decays):
    length = x_head.shape[0]
    blocks = length // BLOCK
    x_part = x_head.reshape(blocks, BLOCK, -1).astype(jnp.float32)
    b_part = b_head.reshape(blocks, BLOCK, -1).astype(jnp.float32)
    c_part = c_head.reshape(blocks, BLOCK, -1).astype(jnp.float32)
    rate_part = rates.reshape(blocks, BLOCK)
    log_decay = jnp.cumsum(decays.reshape(blocks, BLOCK), axis=1)
    causal = jnp.arange(BLOCK)[:, None] >= jnp.arange(BLOCK)[None, :]
    scores = jnp.einsum('cin,cjn->cij', c_part, b_part, precision=lax.Precision.HIGHEST)
    spread = jnp.where(causal, log_decay[:, :, None] - log_decay[:, None, :], 0.0)
    mixing = jnp.where(causal, scores * jnp.exp(spread) * rate_part[:, None, :], 0.0).astype(jnp.bfloat16)
    mixing = lax.optimization_barrier(mixing).astype(jnp.float32)
    inner = jnp.einsum('cij,cjp->cip', mixing, x_part, precision=lax.Precision.HIGHEST)
    weighted_b = (b_part * (jnp.exp(log_decay[:, -1:] - log_decay) * rate_part)[:, :, None]).astype(jnp.bfloat16)
    weighted_b = lax.optimization_barrier(weighted_b).astype(jnp.float32)
    block_states = jnp.einsum('cjn,cjp->cnp', weighted_b, x_part, precision=lax.Precision.HIGHEST)
    totals = log_decay[:, -1]

    def carry_step(state, pair):
        total, fresh = pair
        return (jnp.exp(total) * state + fresh, state)
    final_state, entering = lax.scan(carry_step, jnp.zeros(block_states.shape[1:], jnp.float32), (totals, block_states))
    entering_low = lax.optimization_barrier(entering.astype(jnp.bfloat16)).astype(jnp.float32)
    outer = jnp.exp(log_decay)[:, :, None] * jnp.einsum('cin,cnp->cip', c_part, entering_low, precision=lax.Precision.HIGHEST)
    return (inner + outer).reshape(length, -1)

def reference(x_in, b_in, c_in, z_in, dt_raw, dt_bias, a_log, d_skip, conv_x, conv_b, conv_c, norm_gain):
    length = x_in.shape[0]
    x_conv = causal_conv(x_in, conv_x)
    b_conv = causal_conv(b_in, conv_b)
    c_conv = causal_conv(c_in, conv_c)
    rates = jax.nn.softplus(dt_raw.astype(jnp.float32) + dt_bias[None, :])
    decays = rates * (-jnp.exp(a_log))[None, :]
    x_heads = x_conv.reshape(length, HEADS, HEAD_DIM)
    b_groups = b_conv.reshape(length, GROUPS, STATE)
    c_groups = c_conv.reshape(length, GROUPS, STATE)
    per_group = HEADS // GROUPS

    def one_head(head_id):
        group_id = head_id // per_group
        x_head = lax.dynamic_index_in_dim(x_heads, head_id, 1, keepdims=False)
        b_head = lax.dynamic_index_in_dim(b_groups, group_id, 1, keepdims=False)
        c_head = lax.dynamic_index_in_dim(c_groups, group_id, 1, keepdims=False)
        rate_head = lax.dynamic_index_in_dim(rates, head_id, 1, keepdims=False)
        decay_head = lax.dynamic_index_in_dim(decays, head_id, 1, keepdims=False)
        scanned = blockwise_scan(x_head, b_head, c_head, rate_head, decay_head)
        skip_head = lax.dynamic_index_in_dim(d_skip, head_id, 0, keepdims=False)
        return (scanned + skip_head * x_head.astype(jnp.float32)).astype(jnp.bfloat16)
    heads_out = lax.map(one_head, jnp.arange(HEADS, dtype=jnp.int32))
    merged = jnp.transpose(heads_out, (1, 0, 2)).reshape(length, HEADS * HEAD_DIM).astype(jnp.float32)
    gated = merged * jax.nn.silu(z_in.astype(jnp.float32))
    grouped = gated.reshape(length, GROUPS, -1)
    mean_square = lax.optimization_barrier(jnp.mean(grouped * grouped, axis=-1, keepdims=True))
    normed = (grouped * lax.rsqrt(mean_square + 1e-05)).reshape(length, -1)
    return (normed * norm_gain[None, :]).astype(jnp.bfloat16)
```

```python
import functools

import jax
import jax.numpy as jnp
from jax import lax
from jax.experimental import pallas as pl
from jax.experimental.pallas import tpu as pltpu
from jax.sharding import PartitionSpec as P

HEAD_DIM = 64
STATE = 256
BLOCK = 256
LEAD = 16
PAIR = 2 * HEAD_DIM
NT = (((1,), (1,)), ((), ()))
TN = (((0,), (0,)), ((), ()))


def each(count, step):
    if count == 1:
        step(0)
    else:
        lax.fori_loop(0, count, lambda i, c: (step(i), c)[1], 0)


def aligned(index, unit):
    return pl.ds(pl.multiple_of(index * unit, unit), unit)


def conv_into(out_ref, buf_ref, taps_ref, rows, width):
    chunks = width // 128

    def lanes_step(k):
        lanes = aligned(k, 128)
        taps = taps_ref[:, lanes].astype(jnp.float32)
        count = taps.shape[0]
        for r in range(BLOCK // rows):
            part = buf_ref[r * rows : r * rows + rows + LEAD, lanes].astype(jnp.float32)
            total = taps[count - 1 : count] * part[LEAD:]
            for i in range(count - 1):
                total += taps[i : i + 1] * pltpu.roll(part, count - 1 - i, 0)[LEAD:]
            out_ref[r * rows : (r + 1) * rows, lanes] = jax.nn.silu(total).astype(jnp.bfloat16)

    if chunks <= 2:
        for k in range(chunks):
            lanes_step(k)
    else:
        each(chunks, lanes_step)


def kernel(
    blocks, members, rows, per_group, eps,
    x_hbm, b_hbm, c_hbm, z_hbm, dt_hbm, bias, alog, skip, tx_hbm, tb_hbm, tc_hbm, gain_hbm,
    out_ref,
    xbuf, bbuf, cbuf, dtbuf, zbuf, tx, tb, tc, gain,
    xconv, bconv, cconv, rowbuf, colbuf, acc, escale, enter, leave, outgoing, ret,
    local_sem, send_sem, recv_sem, halo_send, halo_recv, state_send, state_recv, ret_send, ret_recv,
):
    place = lax.axis_index("seq")
    me = lax.rem(place, members)
    block = place // members
    base = block * members
    width = per_group * HEAD_DIM
    pairs = per_group // 2
    high, low = me // 2, lax.rem(me, 2)

    def partner(d):
        return lax.rem(high + d // 2, 2) * 2 + lax.rem(low + d % 2, 2)

    def at(index):
        return {"seq": index}

    has_next = block < blocks - 1
    has_prev = block > 0
    is_last = me == members - 1

    barrier = pltpu.get_barrier_semaphore()
    for d in range(1, members):
        pl.semaphore_signal(barrier, inc=1, device_id=at(base + partner(d)))

    @pl.when(has_prev)
    def _():
        pl.semaphore_signal(barrier, inc=1, device_id=at(base - 1))

    @pl.when(jnp.logical_and(has_prev, jnp.logical_not(is_last)))
    def _():
        pl.semaphore_signal(barrier, inc=1, device_id=at(place - members))

    sources = (dt_hbm, x_hbm, b_hbm, c_hbm)
    buffers = (dtbuf, xbuf, bbuf, cbuf)
    widths = (None, width, STATE, STATE)

    def piece(n, group):
        if widths[n] is None:
            return sources[n]
        return sources[n].at[:, aligned(group, widths[n])]

    def slot(n, member):
        if widths[n] is None:
            return buffers[n].at[pl.ds(pl.multiple_of(member * rows, rows), rows)]
        return buffers[n].at[pl.ds(pl.multiple_of(member * rows + LEAD, LEAD), rows)]

    own = [pltpu.make_async_copy(piece(n, me), slot(n, me), local_sem.at[n]) for n in range(4)]
    small = [
        pltpu.make_async_copy(tx_hbm.at[:, aligned(me, width)], tx, local_sem.at[4]),
        pltpu.make_async_copy(tb_hbm.at[:, aligned(me, STATE)], tb, local_sem.at[5]),
        pltpu.make_async_copy(tc_hbm.at[:, aligned(me, STATE)], tc, local_sem.at[6]),
        pltpu.make_async_copy(gain_hbm, gain, local_sem.at[7]),
        pltpu.make_async_copy(z_hbm, zbuf, local_sem.at[8]),
    ]
    for copy in own + small:
        copy.start()

    @pl.when(jnp.logical_not(has_prev))
    def _():
        for buf in (xbuf, bbuf, cbuf):
            buf[0:LEAD] = jnp.zeros((LEAD, buf.shape[1]), jnp.bfloat16)
        enter[...] = jnp.zeros_like(enter)

    next_count = jnp.where(is_last, members, 1)
    pl.semaphore_wait(barrier, members - 1 + jnp.where(has_next, next_count, 0))

    sends = {}
    for n in range(4):
        for d in (3, 2, 1):
            sends[n, d] = pltpu.make_async_remote_copy(
                src_ref=piece(n, partner(d)),
                dst_ref=slot(n, me),
                send_sem=send_sem.at[n, d - 1],
                recv_sem=recv_sem.at[n, d - 1],
                device_id=at(base + partner(d)),
            )

    def halo(n, member):
        return pltpu.make_async_remote_copy(
            src_ref=sources[n].at[rows - LEAD : rows, aligned(member, widths[n])],
            dst_ref=buffers[n].at[0:LEAD],
            send_sem=halo_send.at[n - 1, member],
            recv_sem=halo_recv.at[n - 1],
            device_id=at(base + members + member),
        )

    sends_halo = jnp.logical_and(has_next, is_last)
    for n in range(4):
        for d in (3, 2, 1):
            sends[n, d].start()
        if n > 0:

            @pl.when(sends_halo)
            def _(n=n):
                for member in range(members):
                    halo(n, member).start()

    def arrive(n):
        own[n].wait()
        for d in (1, 2, 3):
            sends[n, d].wait_recv()
        if n > 0:

            @pl.when(has_prev)
            def _():
                halo(n, 0).wait_recv()

    arrive(0)
    raw = jnp.transpose(dtbuf[...].astype(jnp.float32))
    heads_here = raw.shape[0]
    head_id = lax.broadcasted_iota(jnp.int32, (heads_here, BLOCK), 0)
    sub = lax.broadcasted_iota(jnp.int32, (8, BLOCK), 0)
    up_to = (
        lax.broadcasted_iota(jnp.int32, (BLOCK, BLOCK), 0)
        <= lax.broadcasted_iota(jnp.int32, (BLOCK, BLOCK), 1)
    ).astype(jnp.float32).astype(jnp.bfloat16)

    def rates_step(p):
        first = me * per_group + 2 * p

        def row(k):
            return jnp.sum(jnp.where(head_id == first + k, raw, 0.0), axis=0, keepdims=True)

        def both(ref):
            return jnp.where(sub == 0, ref[first], ref[first + 1])

        v = jnp.where(sub == 0, row(0), row(1)) + both(bias)
        rates = jnp.maximum(v, 0.0) + jnp.log1p(jnp.exp(-jnp.abs(v)))
        decays = rates * -jnp.exp(both(alog))
        top = decays.astype(jnp.bfloat16).astype(jnp.float32)
        rest = decays - top
        middle = rest.astype(jnp.bfloat16).astype(jnp.float32)
        stacked = jnp.concatenate([top, middle, rest - middle, jnp.zeros_like(top)], axis=0)
        summed = jnp.dot(stacked.astype(jnp.bfloat16), up_to, preferred_element_type=jnp.float32)
        log_decay = summed[0:8] + summed[8:16] + summed[16:24]
        weight = jnp.exp(log_decay[:, BLOCK - 1 : BLOCK] - log_decay) * rates
        rowbuf[p, 0:8] = log_decay
        rowbuf[p, 8:16] = rates
        colbuf[p] = jnp.transpose(
            jnp.concatenate([log_decay, weight, jnp.exp(log_decay)], axis=0)
        )

    each(pairs, rates_step)

    first_half = lax.broadcasted_iota(jnp.int32, (BLOCK, PAIR), 1) < HEAD_DIM

    def spread(p, column):
        return jnp.where(
            first_half, colbuf[p, :, column : column + 1], colbuf[p, :, column + 1 : column + 2]
        )

    for copy in small[:3]:
        copy.wait()
    arrive(1)
    conv_into(xconv, xbuf, tx, rows, width)
    arrive(2)
    conv_into(bconv, bbuf, tb, rows, STATE)

    carry = pltpu.make_async_remote_copy(
        src_ref=leave,
        dst_ref=enter,
        send_sem=state_send,
        recv_sem=state_recv,
        device_id=at(place + members),
    )

    if blocks > 2:

        @pl.when(has_prev)
        def _():
            carry.wait_recv()

    @pl.when(has_next)
    def _():
        def state_step(p):
            scaled = (xconv[:, aligned(p, PAIR)].astype(jnp.float32) * spread(p, 8)).astype(
                jnp.bfloat16
            )
            fresh = lax.dot_general(scaled, bconv[...], TN, preferred_element_type=jnp.float32)
            if blocks > 2:
                total = jnp.exp(rowbuf[p, 0:8, BLOCK - 1 : BLOCK])
                upper = lax.broadcasted_iota(jnp.int32, (PAIR, STATE), 0) < HEAD_DIM
                fresh += jnp.where(upper, total[0:1], total[1:2]) * enter[aligned(p, PAIR)]
            leave[aligned(p, PAIR)] = fresh.astype(leave.dtype)

        each(pairs, state_step)
        carry.start()

    arrive(3)
    conv_into(cconv, cbuf, tc, rows, STATE)
    scores = lax.dot_general(cconv[...], bconv[...], NT, preferred_element_type=jnp.float32)
    causal = lax.broadcasted_iota(jnp.int32, (BLOCK, BLOCK), 0) >= lax.broadcasted_iota(
        jnp.int32, (BLOCK, BLOCK), 1
    )

    def inner_step(p):
        x_pair = xconv[:, aligned(p, PAIR)]
        x_wide = x_pair.astype(jnp.float32)
        first = me * per_group + 2 * p
        total = jnp.where(first_half, skip[first], skip[first + 1]) * x_wide
        for k in range(2):
            gap = colbuf[p, :, k : k + 1] - rowbuf[p, k : k + 1]
            mixing = jnp.where(
                causal,
                scores * jnp.exp(jnp.where(causal, gap, 0.0)) * rowbuf[p, 8 + k : 9 + k],
                0.0,
            ).astype(jnp.bfloat16)
            mine = first_half if k == 0 else jnp.logical_not(first_half)
            x_mine = jnp.where(mine, x_wide, 0.0).astype(jnp.bfloat16)
            total += jnp.dot(mixing, x_mine, preferred_element_type=jnp.float32)
        acc[:, aligned(p, PAIR)] = total
        escale[:, aligned(p, PAIR)] = spread(p, 16)

    each(pairs, inner_step)

    if blocks == 2:

        @pl.when(has_prev)
        def _():
            carry.wait_recv()

    returns = {}
    for d in (3, 2, 1, 0):
        target = partner(d)
        here = pl.ds(pl.multiple_of(target * rows, rows), rows)
        outer = lax.dot_general(
            cconv[here], enter[...].astype(jnp.bfloat16), NT, preferred_element_type=jnp.float32
        )
        result = (acc[here] + escale[here] * outer).astype(jnp.bfloat16)
        if d == 0:
            ret[me] = result
        else:
            outgoing[d - 1] = result
            returns[d] = pltpu.make_async_remote_copy(
                src_ref=outgoing.at[d - 1],
                dst_ref=ret.at[me],
                send_sem=ret_send.at[d - 1],
                recv_sem=ret_recv.at[d - 1],
                device_id=at(base + target),
            )
            returns[d].start()

    for copy in small[3:]:
        copy.wait()
    for n in range(4):
        for d in (1, 2, 3):
            sends[n, d].wait_send()

    @pl.when(sends_halo)
    def _():
        for n in (1, 2, 3):
            for member in range(members):
                halo(n, member).wait_send()

    @pl.when(has_next)
    def _():
        carry.wait_send()

    for d in (1, 2, 3):
        returns[d].wait_send()
        returns[d].wait_recv()

    for group in range(members):
        lanes = slice(group * width, (group + 1) * width)
        gated = ret[group].astype(jnp.float32) * jax.nn.silu(zbuf[:, lanes].astype(jnp.float32))
        mean_square = jnp.sum(gated * gated, axis=-1, keepdims=True) * (1.0 / width)
        out_ref[:, lanes] = (gated * lax.rsqrt(mean_square + eps) * gain[:, lanes]).astype(
            jnp.bfloat16
        )


def body(x_in, b_in, c_in, z_in, dt_raw, dt_bias, a_log, d_skip, conv_x, conv_b, conv_c, norm_gain):
    rows, channels = x_in.shape
    heads_here = dt_raw.shape[1]
    groups_here = b_in.shape[1] // STATE
    per_group = heads_here // groups_here
    members = BLOCK // rows
    blocks = lax.axis_size("seq") // members
    assert members == 4 and groups_here == members and per_group % 2 == 0
    width = per_group * HEAD_DIM
    pairs = per_group // 2
    taps = conv_x.shape[0]
    carried = jnp.bfloat16 if blocks == 2 else jnp.float32
    low, full = jnp.bfloat16, jnp.float32
    dma = pltpu.SemaphoreType.DMA
    hbm = pl.BlockSpec(memory_space=pl.ANY)
    smem = pl.BlockSpec(memory_space=pltpu.SMEM)
    return pl.pallas_call(
        functools.partial(kernel, blocks, members, rows, per_group, 1e-5),
        out_shape=jax.ShapeDtypeStruct((rows, channels), jnp.bfloat16),
        in_specs=[hbm] * 5 + [smem] * 3 + [hbm] * 4,
        out_specs=pl.BlockSpec(memory_space=pltpu.VMEM),
        scratch_shapes=[
            pltpu.VMEM((LEAD + BLOCK, width), low),
            pltpu.VMEM((LEAD + BLOCK, STATE), low),
            pltpu.VMEM((LEAD + BLOCK, STATE), low),
            pltpu.VMEM((BLOCK, heads_here), low),
            pltpu.VMEM((rows, channels), low),
            pltpu.VMEM((taps, width), low),
            pltpu.VMEM((taps, STATE), low),
            pltpu.VMEM((taps, STATE), low),
            pltpu.VMEM((1, channels), full),
            pltpu.VMEM((BLOCK, width), low),
            pltpu.VMEM((BLOCK, STATE), low),
            pltpu.VMEM((BLOCK, STATE), low),
            pltpu.VMEM((pairs, 16, BLOCK), full),
            pltpu.VMEM((pairs, BLOCK, 24), full),
            pltpu.VMEM((BLOCK, width), full),
            pltpu.VMEM((BLOCK, width), full),
            pltpu.VMEM((width, STATE), carried),
            pltpu.VMEM((width, STATE), carried),
            pltpu.VMEM((members - 1, rows, width), low),
            pltpu.VMEM((members, rows, width), low),
            dma((9,)),
            dma((4, 3)),
            dma((4, 3)),
            dma((3, members)),
            dma((3,)),
            dma,
            dma,
            dma((3,)),
            dma((3,)),
        ],
        compiler_params=pltpu.CompilerParams(
            collective_id=0, has_side_effects=True, vmem_limit_bytes=48 * 1024 * 1024
        ),
    )(
        x_in, b_in, c_in, z_in, dt_raw, dt_bias, a_log, d_skip,
        conv_x, conv_b, conv_c, norm_gain.reshape(1, channels),
    )


def solution(mesh):
    placed = (
        P(("rep", "seq"), "head"),
        P(("rep", "seq"), "head"),
        P(("rep", "seq"), "head"),
        P(("rep", "seq"), "head"),
        P(("rep", "seq"), "head"),
        P("head"),
        P("head"),
        P("head"),
        P(None, "head"),
        P(None, "head"),
        P(None, "head"),
        P("head"),
    )
    return jax.shard_map(
        body, mesh=mesh, in_specs=placed, out_specs=P(("rep", "seq"), "head"), check_vma=False
    )
```

```python
import functools

import jax
import jax.numpy as jnp
from jax import lax
from jax.experimental import pallas as pl
from jax.experimental.pallas import tpu as pltpu
from jax.sharding import PartitionSpec as P

HEAD_DIM = 64
STATE = 256
BLOCK = 256
LEAD = 16
PAIR = 2 * HEAD_DIM
NT = (((1,), (1,)), ((), ()))
TN = (((0,), (0,)), ((), ()))


def each(count, step):
    if count == 1:
        step(0)
    else:
        lax.fori_loop(0, count, lambda i, c: (step(i), c)[1], 0)


def aligned(index, unit):
    return pl.ds(pl.multiple_of(index * unit, unit), unit)


def halo_spots(width):
    return [(n, k) for n, w in enumerate((width, STATE, STATE)) for k in range(0, w, 128)]


def halo_tiles(width):
    return -(-len(halo_spots(width)) // 5)


def conv_into(out_ref, buf_ref, taps_ref, rows, width):
    chunks = width // 128

    def lanes_step(k):
        lanes = aligned(k, 128)
        taps = taps_ref[:, lanes].astype(jnp.float32)
        count = taps.shape[0]
        for r in range(BLOCK // rows):
            part = buf_ref[r * rows : r * rows + rows + LEAD, lanes].astype(jnp.float32)
            total = taps[count - 1 : count] * part[LEAD:]
            for i in range(count - 1):
                total += taps[i : i + 1] * pltpu.roll(part, count - 1 - i, 0)[LEAD:]
            out_ref[r * rows : (r + 1) * rows, lanes] = jax.nn.silu(total).astype(jnp.bfloat16)

    if chunks <= 2:
        for k in range(chunks):
            lanes_step(k)
    else:
        each(chunks, lanes_step)


def kernel(
    blocks, members, rows, per_group, eps,
    x_hbm, b_hbm, c_hbm, z_hbm, dt_hbm, bias_hbm, alog_hbm, skip_hbm, tx_hbm, tb_hbm, tc_hbm, gain_hbm,
    out_ref,
    xbuf, bbuf, cbuf, dtbuf, zbuf, tx, tb, tc, gain, bias, alog, skip,
    xtail, btail, ctail, packed, unpacked, gate,
    xconv, bconv, cconv, rowbuf, colbuf, acc, escale, enter, leave, outgoing, ret,
    local_sem, send_sem, recv_sem, halo_send, halo_recv, state_send, state_recv, ret_send, ret_recv,
):
    place = lax.axis_index("seq")
    me = lax.rem(place, members)
    block = place // members
    base = block * members
    width = per_group * HEAD_DIM
    pairs = per_group // 2
    high, low = me // 2, lax.rem(me, 2)

    def partner(d):
        return lax.rem(high + d // 2, 2) * 2 + lax.rem(low + d % 2, 2)

    def at(index):
        return {"seq": index}

    has_next = block < blocks - 1
    has_prev = block > 0
    is_last = me == members - 1

    barrier = pltpu.get_barrier_semaphore()
    for d in range(1, members):
        pl.semaphore_signal(barrier, inc=1, device_id=at(base + partner(d)))

    @pl.when(has_prev)
    def _():
        pl.semaphore_signal(barrier, inc=1, device_id=at(base - 1))

    @pl.when(jnp.logical_and(has_prev, jnp.logical_not(is_last)))
    def _():
        pl.semaphore_signal(barrier, inc=1, device_id=at(place - members))

    sources = (dt_hbm, x_hbm, b_hbm, c_hbm)
    buffers = (dtbuf, xbuf, bbuf, cbuf)
    widths = (None, width, STATE, STATE)

    def piece(n, group):
        if widths[n] is None:
            return sources[n]
        return sources[n].at[:, aligned(group, widths[n])]

    def slot(n, member):
        if widths[n] is None:
            return buffers[n].at[member]
        return buffers[n].at[pl.ds(pl.multiple_of(member * rows + LEAD, LEAD), rows)]

    own = [pltpu.make_async_copy(piece(n, me), slot(n, me), local_sem.at[n]) for n in range(4)]
    small = [
        pltpu.make_async_copy(tx_hbm.at[:, aligned(me, width)], tx, local_sem.at[4]),
        pltpu.make_async_copy(tb_hbm.at[:, aligned(me, STATE)], tb, local_sem.at[5]),
        pltpu.make_async_copy(tc_hbm.at[:, aligned(me, STATE)], tc, local_sem.at[6]),
        pltpu.make_async_copy(gain_hbm, gain, local_sem.at[7]),
        pltpu.make_async_copy(z_hbm, zbuf, local_sem.at[8]),
        pltpu.make_async_copy(bias_hbm, bias, local_sem.at[9]),
        pltpu.make_async_copy(alog_hbm, alog, local_sem.at[10]),
        pltpu.make_async_copy(skip_hbm, skip, local_sem.at[11]),
    ]
    tails = [
        pltpu.make_async_copy(hbm.at[rows - LEAD : rows], tail, local_sem.at[12 + k])
        for k, (hbm, tail) in enumerate(((x_hbm, xtail), (b_hbm, btail), (c_hbm, ctail)))
    ]
    sends_halo = jnp.logical_and(has_next, is_last)

    @pl.when(sends_halo)
    def _():
        for copy in tails:
            copy.start()

    for copy in own + small:
        copy.start()

    @pl.when(jnp.logical_not(has_prev))
    def _():
        for buf in (xbuf, bbuf, cbuf):
            buf[0:LEAD] = jnp.zeros((LEAD, buf.shape[1]), jnp.bfloat16)
        enter[...] = jnp.zeros_like(enter)

    next_count = jnp.where(is_last, members, 1)
    pl.semaphore_wait(barrier, members - 1 + jnp.where(has_next, next_count, 0))

    sends = {}
    for n in range(4):
        for d in (3, 2, 1):
            sends[n, d] = pltpu.make_async_remote_copy(
                src_ref=piece(n, partner(d)),
                dst_ref=slot(n, me),
                send_sem=send_sem.at[n, d - 1],
                recv_sem=recv_sem.at[n, d - 1],
                device_id=at(base + partner(d)),
            )

    def halo(member):
        return pltpu.make_async_remote_copy(
            src_ref=packed.at[member],
            dst_ref=unpacked,
            send_sem=halo_send.at[member],
            recv_sem=halo_recv,
            device_id=at(base + members + member),
        )

    for n in range(4):
        for d in (3, 2, 1):
            sends[n, d].start()

    spots = halo_spots(width)
    inside = lax.broadcasted_iota(jnp.int32, (LEAD, 128), 0)

    @pl.when(sends_halo)
    def _():
        for copy in tails:
            copy.wait()
        for member in range(members):
            tile = jnp.zeros((LEAD, 128), jnp.float32)
            for q, (n, start) in enumerate(spots):
                place_in = 3 * (q % 5)
                tail = (xtail, btail, ctail)[n]
                offset = member * (width if n == 0 else STATE) + start
                part = tail[:, offset : offset + 128].astype(jnp.float32)
                part = pltpu.roll(part, (place_in + 3) % LEAD, 0)
                fits = jnp.logical_and(inside >= place_in, inside < place_in + 3)
                tile = jnp.where(fits, part, tile)
                if q % 5 == 4 or q == len(spots) - 1:
                    first = q // 5 * LEAD
                    packed[member, first : first + LEAD] = tile.astype(jnp.bfloat16)
            halo(member).start()

    def take_halo():
        @pl.when(has_prev)
        def _():
            halo(0).wait_recv()
            for q, (n, start) in enumerate(spots):
                first = q // 5 * LEAD
                tile = unpacked[first : first + LEAD].astype(jnp.float32)
                part = pltpu.roll(tile, (13 - 3 * (q % 5)) % LEAD, 0)
                buffers[n + 1][0:LEAD, start : start + 128] = part.astype(jnp.bfloat16)

    def arrive(n):
        own[n].wait()
        for d in (1, 2, 3):
            sends[n, d].wait_recv()

    arrive(0)
    raw = jnp.concatenate([dtbuf[m] for m in range(members)], axis=1).astype(jnp.float32)
    for copy in small[5:]:
        copy.wait()
    heads_here = raw.shape[0]
    head_id = lax.broadcasted_iota(jnp.int32, (heads_here, BLOCK), 0)
    sub = lax.broadcasted_iota(jnp.int32, (8, BLOCK), 0)
    up_to = (
        lax.broadcasted_iota(jnp.int32, (BLOCK, BLOCK), 0)
        <= lax.broadcasted_iota(jnp.int32, (BLOCK, BLOCK), 1)
    ).astype(jnp.float32).astype(jnp.bfloat16)

    def rates_step(p):
        first = me * per_group + 2 * p

        def row(k):
            return jnp.sum(jnp.where(head_id == first + k, raw, 0.0), axis=0, keepdims=True)

        def both(ref):
            return jnp.where(sub == 0, ref[first], ref[first + 1])

        v = jnp.where(sub == 0, row(0), row(1)) + both(bias)
        rates = jnp.maximum(v, 0.0) + jnp.log1p(jnp.exp(-jnp.abs(v)))
        decays = rates * -jnp.exp(both(alog))
        top = decays.astype(jnp.bfloat16).astype(jnp.float32)
        rest = decays - top
        middle = rest.astype(jnp.bfloat16).astype(jnp.float32)
        stacked = jnp.concatenate([top, middle, rest - middle, jnp.zeros_like(top)], axis=0)
        summed = jnp.dot(stacked.astype(jnp.bfloat16), up_to, preferred_element_type=jnp.float32)
        log_decay = summed[0:8] + summed[8:16] + summed[16:24]
        weight = jnp.exp(log_decay[:, BLOCK - 1 : BLOCK] - log_decay) * rates
        rowbuf[p, 0:8] = log_decay
        rowbuf[p, 8:16] = rates
        colbuf[p] = jnp.transpose(
            jnp.concatenate([log_decay, weight, jnp.exp(log_decay)], axis=0)
        )

    each(pairs, rates_step)

    first_half = lax.broadcasted_iota(jnp.int32, (BLOCK, PAIR), 1) < HEAD_DIM

    def spread(p, column):
        return jnp.where(
            first_half, colbuf[p, :, column : column + 1], colbuf[p, :, column + 1 : column + 2]
        )

    for copy in small[:3]:
        copy.wait()
    take_halo()
    arrive(1)
    conv_into(xconv, xbuf, tx, rows, width)
    arrive(2)
    conv_into(bconv, bbuf, tb, rows, STATE)

    carry = pltpu.make_async_remote_copy(
        src_ref=leave,
        dst_ref=enter,
        send_sem=state_send,
        recv_sem=state_recv,
        device_id=at(place + members),
    )

    if blocks > 2:

        @pl.when(has_prev)
        def _():
            carry.wait_recv()

    @pl.when(has_next)
    def _():
        def state_step(p):
            scaled = (xconv[:, aligned(p, PAIR)].astype(jnp.float32) * spread(p, 8)).astype(
                jnp.bfloat16
            )
            fresh = lax.dot_general(scaled, bconv[...], TN, preferred_element_type=jnp.float32)
            if blocks > 2:
                total = jnp.exp(rowbuf[p, 0:8, BLOCK - 1 : BLOCK])
                upper = lax.broadcasted_iota(jnp.int32, (PAIR, STATE), 0) < HEAD_DIM
                fresh += jnp.where(upper, total[0:1], total[1:2]) * enter[aligned(p, PAIR)]
            leave[aligned(p, PAIR)] = fresh.astype(leave.dtype)

        each(pairs, state_step)
        carry.start()

    arrive(3)
    conv_into(cconv, cbuf, tc, rows, STATE)
    scores = lax.dot_general(cconv[...], bconv[...], NT, preferred_element_type=jnp.float32)
    causal = lax.broadcasted_iota(jnp.int32, (BLOCK, BLOCK), 0) >= lax.broadcasted_iota(
        jnp.int32, (BLOCK, BLOCK), 1
    )

    def inner_step(p):
        x_pair = xconv[:, aligned(p, PAIR)]
        x_wide = x_pair.astype(jnp.float32)
        first = me * per_group + 2 * p
        total = jnp.where(first_half, skip[first], skip[first + 1]) * x_wide
        for k in range(2):
            gap = colbuf[p, :, k : k + 1] - rowbuf[p, k : k + 1]
            mixing = jnp.where(
                causal,
                scores * jnp.exp(jnp.where(causal, gap, 0.0)) * rowbuf[p, 8 + k : 9 + k],
                0.0,
            ).astype(jnp.bfloat16)
            mine = first_half if k == 0 else jnp.logical_not(first_half)
            x_mine = jnp.where(mine, x_wide, 0.0).astype(jnp.bfloat16)
            total += jnp.dot(mixing, x_mine, preferred_element_type=jnp.float32)
        acc[:, aligned(p, PAIR)] = total
        escale[:, aligned(p, PAIR)] = spread(p, 16)

    each(pairs, inner_step)

    for copy in small[3:5]:
        copy.wait()
    for group in range(members):
        lanes = slice(group * width, (group + 1) * width)
        gate[:, lanes] = jax.nn.silu(zbuf[:, lanes].astype(jnp.float32))

    if blocks == 2:

        @pl.when(has_prev)
        def _():
            carry.wait_recv()

    returns = {}
    for d in (3, 2, 1, 0):
        target = partner(d)
        here = pl.ds(pl.multiple_of(target * rows, rows), rows)
        outer = lax.dot_general(
            cconv[here], enter[...].astype(jnp.bfloat16), NT, preferred_element_type=jnp.float32
        )
        result = (acc[here] + escale[here] * outer).astype(jnp.bfloat16)
        if d == 0:
            ret[me] = result
        else:
            outgoing[d - 1] = result
            returns[d] = pltpu.make_async_remote_copy(
                src_ref=outgoing.at[d - 1],
                dst_ref=ret.at[me],
                send_sem=ret_send.at[d - 1],
                recv_sem=ret_recv.at[d - 1],
                device_id=at(base + target),
            )
            returns[d].start()

    for d in (0, 1, 2, 3):
        if d > 0:
            returns[d].wait_recv()
        group = partner(d)
        lanes = aligned(group, width)
        gated = ret[group].astype(jnp.float32) * gate[:, lanes]
        mean_square = jnp.sum(gated * gated, axis=-1, keepdims=True) * (1.0 / width)
        out_ref[:, lanes] = (gated * lax.rsqrt(mean_square + eps) * gain[:, lanes]).astype(
            jnp.bfloat16
        )

    for n in range(4):
        for d in (1, 2, 3):
            sends[n, d].wait_send()

    @pl.when(sends_halo)
    def _():
        for member in range(members):
            halo(member).wait_send()

    @pl.when(has_next)
    def _():
        carry.wait_send()

    for d in (1, 2, 3):
        returns[d].wait_send()


def body(x_in, b_in, c_in, z_in, dt_raw, dt_bias, a_log, d_skip, conv_x, conv_b, conv_c, norm_gain):
    rows, channels = x_in.shape
    heads_here = dt_raw.shape[1]
    groups_here = b_in.shape[1] // STATE
    per_group = heads_here // groups_here
    members = BLOCK // rows
    blocks = lax.axis_size("seq") // members
    assert members == 4 and groups_here == members and per_group % 2 == 0
    width = per_group * HEAD_DIM
    pairs = per_group // 2
    tiles = halo_tiles(width)
    taps = conv_x.shape[0]
    carried = jnp.bfloat16 if blocks == 2 else jnp.float32
    low, full = jnp.bfloat16, jnp.float32
    dma = pltpu.SemaphoreType.DMA
    hbm = pl.BlockSpec(memory_space=pltpu.HBM)
    return pl.pallas_call(
        functools.partial(kernel, blocks, members, rows, per_group, 1e-5),
        out_shape=jax.ShapeDtypeStruct((rows, channels), jnp.bfloat16),
        in_specs=[hbm] * 12,
        out_specs=pl.BlockSpec(memory_space=pltpu.VMEM),
        scratch_shapes=[
            pltpu.VMEM((LEAD + BLOCK, width), low),
            pltpu.VMEM((LEAD + BLOCK, STATE), low),
            pltpu.VMEM((LEAD + BLOCK, STATE), low),
            pltpu.VMEM((members, heads_here, rows), low),
            pltpu.VMEM((rows, channels), low),
            pltpu.VMEM((taps, width), low),
            pltpu.VMEM((taps, STATE), low),
            pltpu.VMEM((taps, STATE), low),
            pltpu.VMEM((1, channels), full),
            pltpu.SMEM((heads_here,), full),
            pltpu.SMEM((heads_here,), full),
            pltpu.SMEM((heads_here,), full),
            pltpu.VMEM((LEAD, channels), low),
            pltpu.VMEM((LEAD, b_in.shape[1]), low),
            pltpu.VMEM((LEAD, b_in.shape[1]), low),
            pltpu.VMEM((members, tiles * LEAD, 128), low),
            pltpu.VMEM((tiles * LEAD, 128), low),
            pltpu.VMEM((rows, channels), full),
            pltpu.VMEM((BLOCK, width), low),
            pltpu.VMEM((BLOCK, STATE), low),
            pltpu.VMEM((BLOCK, STATE), low),
            pltpu.VMEM((pairs, 16, BLOCK), full),
            pltpu.VMEM((pairs, BLOCK, 24), full),
            pltpu.VMEM((BLOCK, width), full),
            pltpu.VMEM((BLOCK, width), full),
            pltpu.VMEM((width, STATE), carried),
            pltpu.VMEM((width, STATE), carried),
            pltpu.VMEM((members - 1, rows, width), low),
            pltpu.VMEM((members, rows, width), low),
            dma((15,)),
            dma((4, 3)),
            dma((4, 3)),
            dma((members,)),
            dma,
            dma,
            dma,
            dma((3,)),
            dma((3,)),
        ],
        compiler_params=pltpu.CompilerParams(
            collective_id=0, has_side_effects=True, vmem_limit_bytes=64 * 1024 * 1024
        ),
    )(
        x_in, b_in, c_in, z_in, dt_raw.T, dt_bias, a_log, d_skip,
        conv_x, conv_b, conv_c, norm_gain.reshape(1, channels),
    )


def solution(mesh):
    placed = (
        P(("rep", "seq"), "head"),
        P(("rep", "seq"), "head"),
        P(("rep", "seq"), "head"),
        P(("rep", "seq"), "head"),
        P(("rep", "seq"), "head"),
        P("head"),
        P("head"),
        P("head"),
        P(None, "head"),
        P(None, "head"),
        P(None, "head"),
        P("head"),
    )
    return jax.shard_map(
        body, mesh=mesh, in_specs=placed, out_specs=P(("rep", "seq"), "head"), check_vma=False
    )
```

```python
import functools

import jax
import jax.numpy as jnp
from jax import lax
from jax.experimental import pallas as pl
from jax.experimental.pallas import tpu as pltpu
from jax.sharding import PartitionSpec as P

HEAD_DIM = 64
STATE = 256
BLOCK = 256
LEAD = 16
PAIR = 2 * HEAD_DIM
NT = (((1,), (1,)), ((), ()))
TN = (((0,), (0,)), ((), ()))


def each(count, step):
    if count == 1:
        step(0)
    else:
        lax.fori_loop(0, count, lambda i, c: (step(i), c)[1], 0)


def aligned(index, unit):
    return pl.ds(pl.multiple_of(index * unit, unit), unit)


def silu(value):
    half = 0.5 * value
    return half * jnp.tanh(half) + half


def halo_spots(width):
    return [(n, k) for n, w in enumerate((width, STATE, STATE)) for k in range(0, w, 128)]


def halo_tiles(width):
    return -(-len(halo_spots(width)) // 5)


def conv_into(out_ref, buf_ref, taps_ref, rows, width):
    chunks = width // 128

    def lanes_step(k):
        lanes = aligned(k, 128)
        taps = taps_ref[:, lanes].astype(jnp.float32)
        count = taps.shape[0]
        for r in range(BLOCK // rows):
            part = buf_ref[r * rows : r * rows + rows + LEAD, lanes].astype(jnp.float32)
            total = taps[count - 1 : count] * part[LEAD:]
            for i in range(count - 1):
                total += taps[i : i + 1] * pltpu.roll(part, count - 1 - i, 0)[LEAD:]
            out_ref[r * rows : (r + 1) * rows, lanes] = silu(total).astype(jnp.bfloat16)

    if chunks <= 2:
        for k in range(chunks):
            lanes_step(k)
    else:
        each(chunks, lanes_step)


def kernel(
    blocks, members, rows, per_group, eps,
    x_hbm, b_hbm, c_hbm, z_hbm, dt_hbm, bias_hbm, alog_hbm, skip_hbm, tx_hbm, tb_hbm, tc_hbm, gain_hbm,
    out_ref,
    xbuf, bbuf, cbuf, dtbuf, zbuf, tx, tb, tc, gain, bias, alog, skip,
    xtail, btail, ctail, packed, unpacked, gate,
    xconv, bconv, cconv, rowbuf, colbuf, acc, escale, enter, leave, outgoing, ret,
    local_sem, send_sem, recv_sem, halo_send, halo_recv, state_send, state_recv, ret_send, ret_recv,
):
    place = lax.axis_index("seq")
    me = lax.rem(place, members)
    block = place // members
    base = block * members
    width = per_group * HEAD_DIM
    pairs = per_group // 2
    high, low = me // 2, lax.rem(me, 2)

    def partner(d):
        return lax.rem(high + d // 2, 2) * 2 + lax.rem(low + d % 2, 2)

    def at(index):
        return {"seq": index}

    has_next = block < blocks - 1
    has_prev = block > 0
    is_last = me == members - 1

    barrier = pltpu.get_barrier_semaphore()
    for d in range(1, members):
        pl.semaphore_signal(barrier, inc=1, device_id=at(base + partner(d)))

    @pl.when(has_prev)
    def _():
        pl.semaphore_signal(barrier, inc=1, device_id=at(base - 1))

    @pl.when(jnp.logical_and(has_prev, jnp.logical_not(is_last)))
    def _():
        pl.semaphore_signal(barrier, inc=1, device_id=at(place - members))

    sources = (dt_hbm, x_hbm, b_hbm, c_hbm)
    buffers = (dtbuf, xbuf, bbuf, cbuf)
    widths = (None, width, STATE, STATE)

    def piece(n, group):
        if widths[n] is None:
            return sources[n]
        return sources[n].at[:, aligned(group, widths[n])]

    def slot(n, member):
        if widths[n] is None:
            return buffers[n].at[member]
        return buffers[n].at[pl.ds(pl.multiple_of(member * rows + LEAD, LEAD), rows)]

    own = [pltpu.make_async_copy(piece(n, me), slot(n, me), local_sem.at[n]) for n in range(4)]
    small = [
        pltpu.make_async_copy(tx_hbm.at[:, aligned(me, width)], tx, local_sem.at[4]),
        pltpu.make_async_copy(tb_hbm.at[:, aligned(me, STATE)], tb, local_sem.at[5]),
        pltpu.make_async_copy(tc_hbm.at[:, aligned(me, STATE)], tc, local_sem.at[6]),
        pltpu.make_async_copy(gain_hbm, gain, local_sem.at[7]),
        pltpu.make_async_copy(z_hbm, zbuf, local_sem.at[8]),
        pltpu.make_async_copy(bias_hbm, bias, local_sem.at[9]),
        pltpu.make_async_copy(alog_hbm, alog, local_sem.at[10]),
        pltpu.make_async_copy(skip_hbm, skip, local_sem.at[11]),
    ]
    tails = [
        pltpu.make_async_copy(hbm.at[rows - LEAD : rows], tail, local_sem.at[12 + k])
        for k, (hbm, tail) in enumerate(((x_hbm, xtail), (b_hbm, btail), (c_hbm, ctail)))
    ]
    sends_halo = jnp.logical_and(has_next, is_last)

    @pl.when(sends_halo)
    def _():
        for copy in tails:
            copy.start()

    for copy in own + small:
        copy.start()

    @pl.when(jnp.logical_not(has_prev))
    def _():
        for buf in (xbuf, bbuf, cbuf):
            buf[0:LEAD] = jnp.zeros((LEAD, buf.shape[1]), jnp.bfloat16)
        enter[...] = jnp.zeros_like(enter)

    next_count = jnp.where(is_last, members, 1)
    pl.semaphore_wait(barrier, members - 1 + jnp.where(has_next, next_count, 0))

    sends = {}
    for n in range(4):
        for d in (3, 2, 1):
            sends[n, d] = pltpu.make_async_remote_copy(
                src_ref=piece(n, partner(d)),
                dst_ref=slot(n, me),
                send_sem=send_sem.at[n, d - 1],
                recv_sem=recv_sem.at[n, d - 1],
                device_id=at(base + partner(d)),
            )

    def halo(member):
        return pltpu.make_async_remote_copy(
            src_ref=packed.at[member],
            dst_ref=unpacked,
            send_sem=halo_send.at[member],
            recv_sem=halo_recv,
            device_id=at(base + members + member),
        )

    def start(n):
        for d in (3, 2, 1):
            sends[n, d].start()

    for n in range(3):
        start(n)

    @pl.when(jnp.logical_not(has_next))
    def _():
        start(3)

    spots = halo_spots(width)
    inside = lax.broadcasted_iota(jnp.int32, (LEAD, 128), 0)

    @pl.when(sends_halo)
    def _():
        for copy in tails:
            copy.wait()
        for member in range(members):
            tile = jnp.zeros((LEAD, 128), jnp.float32)
            for q, (n, start) in enumerate(spots):
                place_in = 3 * (q % 5)
                tail = (xtail, btail, ctail)[n]
                offset = member * (width if n == 0 else STATE) + start
                part = tail[:, offset : offset + 128].astype(jnp.float32)
                part = pltpu.roll(part, (place_in + 3) % LEAD, 0)
                fits = jnp.logical_and(inside >= place_in, inside < place_in + 3)
                tile = jnp.where(fits, part, tile)
                if q % 5 == 4 or q == len(spots) - 1:
                    first = q // 5 * LEAD
                    packed[member, first : first + LEAD] = tile.astype(jnp.bfloat16)
            halo(member).start()

    def take_halo():
        @pl.when(has_prev)
        def _():
            halo(0).wait_recv()
            for q, (n, start) in enumerate(spots):
                first = q // 5 * LEAD
                tile = unpacked[first : first + LEAD].astype(jnp.float32)
                part = pltpu.roll(tile, (13 - 3 * (q % 5)) % LEAD, 0)
                buffers[n + 1][0:LEAD, start : start + 128] = part.astype(jnp.bfloat16)

    def arrive(n):
        own[n].wait()
        for d in (1, 2, 3):
            sends[n, d].wait_recv()

    arrive(0)
    raw = jnp.concatenate([dtbuf[m] for m in range(members)], axis=1).astype(jnp.float32)
    for copy in small[5:]:
        copy.wait()
    heads_here = raw.shape[0]
    head_id = lax.broadcasted_iota(jnp.int32, (heads_here, BLOCK), 0)
    sub = lax.broadcasted_iota(jnp.int32, (8, BLOCK), 0)
    up_to = (
        lax.broadcasted_iota(jnp.int32, (BLOCK, BLOCK), 0)
        <= lax.broadcasted_iota(jnp.int32, (BLOCK, BLOCK), 1)
    ).astype(jnp.float32).astype(jnp.bfloat16)

    def rates_step(p):
        first = me * per_group + 2 * p

        def row(k):
            return jnp.sum(jnp.where(head_id == first + k, raw, 0.0), axis=0, keepdims=True)

        def both(ref):
            return jnp.where(sub == 0, ref[first], ref[first + 1])

        v = jnp.where(sub == 0, row(0), row(1)) + both(bias)
        rates = jnp.maximum(v, 0.0) + jnp.log1p(jnp.exp(-jnp.abs(v)))
        decays = rates * -jnp.exp(both(alog))
        top = decays.astype(jnp.bfloat16).astype(jnp.float32)
        rest = decays - top
        middle = rest.astype(jnp.bfloat16).astype(jnp.float32)
        stacked = jnp.concatenate([top, middle, rest - middle, jnp.zeros_like(top)], axis=0)
        summed = jnp.dot(stacked.astype(jnp.bfloat16), up_to, preferred_element_type=jnp.float32)
        log_decay = summed[0:8] + summed[8:16] + summed[16:24]
        weight = jnp.exp(log_decay[:, BLOCK - 1 : BLOCK] - log_decay) * rates
        rowbuf[p, 0:8] = log_decay
        rowbuf[p, 8:16] = rates
        colbuf[p] = jnp.transpose(
            jnp.concatenate([log_decay, weight, jnp.exp(log_decay)], axis=0)
        )

    each(pairs, rates_step)

    first_half = lax.broadcasted_iota(jnp.int32, (BLOCK, PAIR), 1) < HEAD_DIM

    def spread(p, column):
        return jnp.where(
            first_half, colbuf[p, :, column : column + 1], colbuf[p, :, column + 1 : column + 2]
        )

    for copy in small[:3]:
        copy.wait()
    take_halo()
    arrive(1)
    conv_into(xconv, xbuf, tx, rows, width)
    arrive(2)

    @pl.when(has_next)
    def _():
        start(3)

    conv_into(bconv, bbuf, tb, rows, STATE)

    carry = pltpu.make_async_remote_copy(
        src_ref=leave,
        dst_ref=enter,
        send_sem=state_send,
        recv_sem=state_recv,
        device_id=at(place + members),
    )

    if blocks > 2:

        @pl.when(has_prev)
        def _():
            carry.wait_recv()

    @pl.when(has_next)
    def _():
        def state_step(p):
            scaled = (xconv[:, aligned(p, PAIR)].astype(jnp.float32) * spread(p, 8)).astype(
                jnp.bfloat16
            )
            fresh = lax.dot_general(scaled, bconv[...], TN, preferred_element_type=jnp.float32)
            if blocks > 2:
                total = jnp.exp(rowbuf[p, 0:8, BLOCK - 1 : BLOCK])
                upper = lax.broadcasted_iota(jnp.int32, (PAIR, STATE), 0) < HEAD_DIM
                fresh += jnp.where(upper, total[0:1], total[1:2]) * enter[aligned(p, PAIR)]
            leave[aligned(p, PAIR)] = fresh.astype(leave.dtype)

        each(pairs, state_step)
        carry.start()

    arrive(3)
    conv_into(cconv, cbuf, tc, rows, STATE)
    half = BLOCK // 2
    bands = []
    for r in range(2):
        span, reach = slice(r * half, (r + 1) * half), (r + 1) * half
        scores = lax.dot_general(
            cconv[span], bconv[0:reach], NT, preferred_element_type=jnp.float32
        )
        causal = lax.broadcasted_iota(jnp.int32, (half, reach), 0) + r * half >= (
            lax.broadcasted_iota(jnp.int32, (half, reach), 1)
        )
        bands.append((span, reach, scores, causal))

    def inner_step(p):
        x_pair = xconv[:, aligned(p, PAIR)]
        x_wide = x_pair.astype(jnp.float32)
        first = me * per_group + 2 * p
        direct = jnp.where(first_half, skip[first], skip[first + 1]) * x_wide
        x_mine = [
            jnp.where(mine, x_wide, 0.0).astype(jnp.bfloat16)
            for mine in (first_half, jnp.logical_not(first_half))
        ]
        for span, reach, scores, causal in bands:
            total = direct[span]
            for k in range(2):
                gap = colbuf[p, span, k : k + 1] - rowbuf[p, k : k + 1, 0:reach]
                mixing = jnp.where(
                    causal,
                    scores
                    * jnp.exp(jnp.where(causal, gap, 0.0))
                    * rowbuf[p, 8 + k : 9 + k, 0:reach],
                    0.0,
                ).astype(jnp.bfloat16)
                total += jnp.dot(mixing, x_mine[k][0:reach], preferred_element_type=jnp.float32)
            acc[span, aligned(p, PAIR)] = total
        escale[:, aligned(p, PAIR)] = spread(p, 16)

    each(pairs, inner_step)

    for copy in small[3:5]:
        copy.wait()
    for group in range(members):
        lanes = slice(group * width, (group + 1) * width)
        gate[:, lanes] = silu(zbuf[:, lanes].astype(jnp.float32))

    if blocks == 2:

        @pl.when(has_prev)
        def _():
            carry.wait_recv()

    returns = {}
    for d in (3, 2, 1, 0):
        target = partner(d)
        here = pl.ds(pl.multiple_of(target * rows, rows), rows)
        outer = lax.dot_general(
            cconv[here], enter[...].astype(jnp.bfloat16), NT, preferred_element_type=jnp.float32
        )
        result = (acc[here] + escale[here] * outer).astype(jnp.bfloat16)
        if d == 0:
            ret[me] = result
        else:
            outgoing[d - 1] = result
            returns[d] = pltpu.make_async_remote_copy(
                src_ref=outgoing.at[d - 1],
                dst_ref=ret.at[me],
                send_sem=ret_send.at[d - 1],
                recv_sem=ret_recv.at[d - 1],
                device_id=at(base + target),
            )
            returns[d].start()

    for d in (0, 1, 2, 3):
        if d > 0:
            returns[d].wait_recv()
        group = partner(d)
        lanes = aligned(group, width)
        gated = ret[group].astype(jnp.float32) * gate[:, lanes]
        mean_square = jnp.sum(gated * gated, axis=-1, keepdims=True) * (1.0 / width)
        out_ref[:, lanes] = (gated * lax.rsqrt(mean_square + eps) * gain[:, lanes]).astype(
            jnp.bfloat16
        )

    for n in range(4):
        for d in (1, 2, 3):
            sends[n, d].wait_send()

    @pl.when(sends_halo)
    def _():
        for member in range(members):
            halo(member).wait_send()

    @pl.when(has_next)
    def _():
        carry.wait_send()

    for d in (1, 2, 3):
        returns[d].wait_send()


def body(x_in, b_in, c_in, z_in, dt_raw, dt_bias, a_log, d_skip, conv_x, conv_b, conv_c, norm_gain):
    rows, channels = x_in.shape
    heads_here = dt_raw.shape[1]
    groups_here = b_in.shape[1] // STATE
    per_group = heads_here // groups_here
    members = BLOCK // rows
    blocks = lax.axis_size("seq") // members
    assert members == 4 and groups_here == members and per_group % 2 == 0
    width = per_group * HEAD_DIM
    pairs = per_group // 2
    tiles = halo_tiles(width)
    taps = conv_x.shape[0]
    carried = jnp.bfloat16 if blocks == 2 else jnp.float32
    low, full = jnp.bfloat16, jnp.float32
    dma = pltpu.SemaphoreType.DMA
    hbm = pl.BlockSpec(memory_space=pltpu.HBM)
    operands = [
        pltpu.with_memory_space_constraint(value, pltpu.HBM)
        for value in (
            x_in, b_in, c_in, z_in, dt_raw.T, dt_bias, a_log, d_skip,
            conv_x, conv_b, conv_c, norm_gain.reshape(1, channels),
        )
    ]
    return pl.pallas_call(
        functools.partial(kernel, blocks, members, rows, per_group, 1e-5),
        out_shape=jax.ShapeDtypeStruct((rows, channels), jnp.bfloat16),
        in_specs=[hbm] * 12,
        out_specs=pl.BlockSpec(memory_space=pltpu.VMEM),
        scratch_shapes=[
            pltpu.VMEM((LEAD + BLOCK, width), low),
            pltpu.VMEM((LEAD + BLOCK, STATE), low),
            pltpu.VMEM((LEAD + BLOCK, STATE), low),
            pltpu.VMEM((members, heads_here, rows), low),
            pltpu.VMEM((rows, channels), low),
            pltpu.VMEM((taps, width), low),
            pltpu.VMEM((taps, STATE), low),
            pltpu.VMEM((taps, STATE), low),
            pltpu.VMEM((1, channels), full),
            pltpu.SMEM((heads_here,), full),
            pltpu.SMEM((heads_here,), full),
            pltpu.SMEM((heads_here,), full),
            pltpu.VMEM((LEAD, channels), low),
            pltpu.VMEM((LEAD, b_in.shape[1]), low),
            pltpu.VMEM((LEAD, b_in.shape[1]), low),
            pltpu.VMEM((members, tiles * LEAD, 128), low),
            pltpu.VMEM((tiles * LEAD, 128), low),
            pltpu.VMEM((rows, channels), full),
            pltpu.VMEM((BLOCK, width), low),
            pltpu.VMEM((BLOCK, STATE), low),
            pltpu.VMEM((BLOCK, STATE), low),
            pltpu.VMEM((pairs, 16, BLOCK), full),
            pltpu.VMEM((pairs, BLOCK, 24), full),
            pltpu.VMEM((BLOCK, width), full),
            pltpu.VMEM((BLOCK, width), full),
            pltpu.VMEM((width, STATE), carried),
            pltpu.VMEM((width, STATE), carried),
            pltpu.VMEM((members - 1, rows, width), low),
            pltpu.VMEM((members, rows, width), low),
            dma((15,)),
            dma((4, 3)),
            dma((4, 3)),
            dma((members,)),
            dma,
            dma,
            dma,
            dma((3,)),
            dma((3,)),
        ],
        compiler_params=pltpu.CompilerParams(
            collective_id=0, has_side_effects=True, vmem_limit_bytes=32 * 1024 * 1024
        ),
    )(
        *operands,
    )


def solution(mesh):
    placed = (
        P(("rep", "seq"), "head"),
        P(("rep", "seq"), "head"),
        P(("rep", "seq"), "head"),
        P(("rep", "seq"), "head"),
        P(("rep", "seq"), "head"),
        P("head"),
        P("head"),
        P("head"),
        P(None, "head"),
        P(None, "head"),
        P(None, "head"),
        P("head"),
    )
    return jax.shard_map(
        body, mesh=mesh, in_specs=placed, out_specs=P(("rep", "seq"), "head"), check_vma=False
    )
```

```python
import functools

import jax
import jax.numpy as jnp
from jax import lax
from jax.experimental import pallas as pl
from jax.experimental.pallas import tpu as pltpu
from jax.sharding import PartitionSpec as P

HEAD_DIM = 64
STATE = 256
BLOCK = 256
LEAD = 16
PAIR = 2 * HEAD_DIM
NT = (((1,), (1,)), ((), ()))
TN = (((0,), (0,)), ((), ()))


def each(count, step):
    if count == 1:
        step(0)
    else:
        lax.fori_loop(0, count, lambda i, c: (step(i), c)[1], 0)


def aligned(index, unit):
    return pl.ds(pl.multiple_of(index * unit, unit), unit)


def silu(value):
    half = 0.5 * value
    return half * jnp.tanh(half) + half


def halo_spots(width):
    return [(n, k) for n, w in enumerate((width, STATE, STATE)) for k in range(0, w, 128)]


def halo_tiles(width):
    return -(-len(halo_spots(width)) // 5)


def conv_into(out_ref, buf_ref, taps_ref, rows, width):
    chunks = width // 128

    def lanes_step(k):
        lanes = aligned(k, 128)
        taps = taps_ref[:, lanes].astype(jnp.float32)
        count = taps.shape[0]
        for r in range(BLOCK // rows):
            part = buf_ref[r * rows : r * rows + rows + LEAD, lanes].astype(jnp.float32)
            total = taps[count - 1 : count] * part[LEAD:]
            for i in range(count - 1):
                total += taps[i : i + 1] * pltpu.roll(part, count - 1 - i, 0)[LEAD:]
            out_ref[r * rows : (r + 1) * rows, lanes] = silu(total).astype(jnp.bfloat16)

    if chunks <= 2:
        for k in range(chunks):
            lanes_step(k)
    else:
        each(chunks, lanes_step)


def kernel(
    blocks, members, rows, per_group, eps,
    x_hbm, b_hbm, c_hbm, z_hbm, dt_hbm, bias_hbm, alog_hbm, skip_hbm, tx_hbm, tb_hbm, tc_hbm, gain_hbm,
    out_ref,
    xbuf, bbuf, cbuf, dtbuf, zbuf, tx, tb, tc, gain, bias, alog, skip,
    xtail, btail, ctail, packed, unpacked, gate,
    xconv, bconv, cconv, rowbuf, colbuf, acc, escale, decay, enter, leave, outgoing, ret,
    local_sem, send_sem, recv_sem, halo_send, halo_recv, state_send, state_recv, ret_send, ret_recv,
):
    place = lax.axis_index("seq")
    me = lax.rem(place, members)
    block = place // members
    base = block * members
    width = per_group * HEAD_DIM
    pairs = per_group // 2
    high, low = me // 2, lax.rem(me, 2)

    def partner(d):
        return lax.rem(high + d // 2, 2) * 2 + lax.rem(low + d % 2, 2)

    def at(index):
        return {"seq": index}

    has_next = block < blocks - 1
    has_prev = block > 0
    is_last = me == members - 1

    barrier = pltpu.get_barrier_semaphore()
    for d in range(1, members):
        pl.semaphore_signal(barrier, inc=1, device_id=at(base + partner(d)))

    @pl.when(has_prev)
    def _():
        pl.semaphore_signal(barrier, inc=1, device_id=at(base - 1))

    @pl.when(jnp.logical_and(has_prev, jnp.logical_not(is_last)))
    def _():
        pl.semaphore_signal(barrier, inc=1, device_id=at(place - members))

    sources = (dt_hbm, x_hbm, b_hbm, c_hbm)
    buffers = (dtbuf, xbuf, bbuf, cbuf)
    widths = (None, width, STATE, STATE)

    def piece(n, group):
        if widths[n] is None:
            return sources[n]
        return sources[n].at[:, aligned(group, widths[n])]

    def slot(n, member):
        if widths[n] is None:
            return buffers[n].at[member]
        return buffers[n].at[pl.ds(pl.multiple_of(member * rows + LEAD, LEAD), rows)]

    own = [pltpu.make_async_copy(piece(n, me), slot(n, me), local_sem.at[n]) for n in range(4)]
    small = [
        pltpu.make_async_copy(tx_hbm.at[:, aligned(me, width)], tx, local_sem.at[4]),
        pltpu.make_async_copy(tb_hbm.at[:, aligned(me, STATE)], tb, local_sem.at[5]),
        pltpu.make_async_copy(tc_hbm.at[:, aligned(me, STATE)], tc, local_sem.at[6]),
        pltpu.make_async_copy(gain_hbm, gain, local_sem.at[7]),
        pltpu.make_async_copy(z_hbm, zbuf, local_sem.at[8]),
        pltpu.make_async_copy(bias_hbm, bias, local_sem.at[9]),
        pltpu.make_async_copy(alog_hbm, alog, local_sem.at[10]),
        pltpu.make_async_copy(skip_hbm, skip, local_sem.at[11]),
    ]
    tails = [
        pltpu.make_async_copy(hbm.at[rows - LEAD : rows], tail, local_sem.at[12 + k])
        for k, (hbm, tail) in enumerate(((x_hbm, xtail), (b_hbm, btail), (c_hbm, ctail)))
    ]
    sends_halo = jnp.logical_and(has_next, is_last)

    @pl.when(sends_halo)
    def _():
        for copy in tails:
            copy.start()

    for copy in own + small:
        copy.start()

    @pl.when(jnp.logical_not(has_prev))
    def _():
        for buf in (xbuf, bbuf, cbuf):
            buf[0:LEAD] = jnp.zeros((LEAD, buf.shape[1]), jnp.bfloat16)
        enter[...] = jnp.zeros_like(enter)

    next_count = jnp.where(is_last, members, 1)
    pl.semaphore_wait(barrier, members - 1 + jnp.where(has_next, next_count, 0))

    sends = {}
    for n in range(4):
        for d in (3, 2, 1):
            sends[n, d] = pltpu.make_async_remote_copy(
                src_ref=piece(n, partner(d)),
                dst_ref=slot(n, me),
                send_sem=send_sem.at[n, d - 1],
                recv_sem=recv_sem.at[n, d - 1],
                device_id=at(base + partner(d)),
            )

    def halo(member):
        return pltpu.make_async_remote_copy(
            src_ref=packed.at[member],
            dst_ref=unpacked,
            send_sem=halo_send.at[member],
            recv_sem=halo_recv,
            device_id=at(base + members + member),
        )

    def start(n):
        for d in (3, 2, 1):
            sends[n, d].start()

    for n in range(3):
        start(n)

    @pl.when(jnp.logical_not(has_next))
    def _():
        start(3)

    spots = halo_spots(width)
    inside = lax.broadcasted_iota(jnp.int32, (LEAD, 128), 0)

    @pl.when(sends_halo)
    def _():
        for copy in tails:
            copy.wait()
        for member in range(members):
            tile = jnp.zeros((LEAD, 128), jnp.float32)
            for q, (n, start) in enumerate(spots):
                place_in = 3 * (q % 5)
                tail = (xtail, btail, ctail)[n]
                offset = member * (width if n == 0 else STATE) + start
                part = tail[:, offset : offset + 128].astype(jnp.float32)
                part = pltpu.roll(part, (place_in + 3) % LEAD, 0)
                fits = jnp.logical_and(inside >= place_in, inside < place_in + 3)
                tile = jnp.where(fits, part, tile)
                if q % 5 == 4 or q == len(spots) - 1:
                    first = q // 5 * LEAD
                    packed[member, first : first + LEAD] = tile.astype(jnp.bfloat16)
            halo(member).start()

    def take_halo():
        @pl.when(has_prev)
        def _():
            halo(0).wait_recv()
            for q, (n, start) in enumerate(spots):
                first = q // 5 * LEAD
                tile = unpacked[first : first + LEAD].astype(jnp.float32)
                part = pltpu.roll(tile, (13 - 3 * (q % 5)) % LEAD, 0)
                buffers[n + 1][0:LEAD, start : start + 128] = part.astype(jnp.bfloat16)

    def arrive(n):
        own[n].wait()
        for d in (1, 2, 3):
            sends[n, d].wait_recv()

    arrive(0)
    raw = jnp.concatenate([dtbuf[m] for m in range(members)], axis=1).astype(jnp.float32)
    for copy in small[5:]:
        copy.wait()
    heads_here = raw.shape[0]
    head_id = lax.broadcasted_iota(jnp.int32, (heads_here, BLOCK), 0)
    sub = lax.broadcasted_iota(jnp.int32, (8, BLOCK), 0)
    up_to = (
        lax.broadcasted_iota(jnp.int32, (BLOCK, BLOCK), 0)
        <= lax.broadcasted_iota(jnp.int32, (BLOCK, BLOCK), 1)
    ).astype(jnp.float32).astype(jnp.bfloat16)

    def rates_step(p):
        first = me * per_group + 2 * p

        def row(k):
            return jnp.sum(jnp.where(head_id == first + k, raw, 0.0), axis=0, keepdims=True)

        def both(ref):
            return jnp.where(sub == 0, ref[first], ref[first + 1])

        v = jnp.where(sub == 0, row(0), row(1)) + both(bias)
        rates = jnp.maximum(v, 0.0) + jnp.log1p(jnp.exp(-jnp.abs(v)))
        decays = rates * -jnp.exp(both(alog))
        top = decays.astype(jnp.bfloat16).astype(jnp.float32)
        rest = decays - top
        middle = rest.astype(jnp.bfloat16).astype(jnp.float32)
        stacked = jnp.concatenate([top, middle, rest - middle, jnp.zeros_like(top)], axis=0)
        summed = jnp.dot(stacked.astype(jnp.bfloat16), up_to, preferred_element_type=jnp.float32)
        log_decay = summed[0:8] + summed[8:16] + summed[16:24]
        weight = jnp.exp(log_decay[:, BLOCK - 1 : BLOCK] - log_decay) * rates
        rowbuf[p, 0:8] = log_decay
        rowbuf[p, 8:16] = rates
        colbuf[p] = jnp.transpose(
            jnp.concatenate([log_decay, weight, jnp.exp(log_decay)], axis=0)
        )

    half = BLOCK // 2
    bands = []
    for r in range(2):
        span, reach = slice(r * half, (r + 1) * half), (r + 1) * half
        causal = lax.broadcasted_iota(jnp.int32, (half, reach), 0) + r * half >= (
            lax.broadcasted_iota(jnp.int32, (half, reach), 1)
        )
        bands.append((span, reach, causal))

    first_half = lax.broadcasted_iota(jnp.int32, (BLOCK, PAIR), 1) < HEAD_DIM

    def spread(p, column):
        return jnp.where(
            first_half, colbuf[p, :, column : column + 1], colbuf[p, :, column + 1 : column + 2]
        )

    def decay_step(p):
        for span, reach, causal in bands:
            for k in range(2):
                gap = colbuf[p, span, k : k + 1] - rowbuf[p, k : k + 1, 0:reach]
                decay[2 * p + k, span, 0:reach] = jnp.where(
                    causal,
                    jnp.exp(jnp.where(causal, gap, 0.0)) * rowbuf[p, 8 + k : 9 + k, 0:reach],
                    0.0,
                )
        escale[:, aligned(p, PAIR)] = spread(p, 16)

    each(pairs, rates_step)
    each(pairs, decay_step)
    for copy in small[3:5]:
        copy.wait()
    for group in range(members):
        lanes = slice(group * width, (group + 1) * width)
        gate[:, lanes] = silu(zbuf[:, lanes].astype(jnp.float32))

    for copy in small[:3]:
        copy.wait()
    take_halo()
    arrive(1)

    @pl.when(has_next)
    def _():
        start(3)

    conv_into(xconv, xbuf, tx, rows, width)
    arrive(2)
    conv_into(bconv, bbuf, tb, rows, STATE)

    carry = pltpu.make_async_remote_copy(
        src_ref=leave,
        dst_ref=enter,
        send_sem=state_send,
        recv_sem=state_recv,
        device_id=at(place + members),
    )

    if blocks > 2:

        @pl.when(has_prev)
        def _():
            carry.wait_recv()

    @pl.when(has_next)
    def _():
        def state_step(p):
            scaled = (xconv[:, aligned(p, PAIR)].astype(jnp.float32) * spread(p, 8)).astype(
                jnp.bfloat16
            )
            fresh = lax.dot_general(scaled, bconv[...], TN, preferred_element_type=jnp.float32)
            if blocks > 2:
                total = jnp.exp(rowbuf[p, 0:8, BLOCK - 1 : BLOCK])
                upper = lax.broadcasted_iota(jnp.int32, (PAIR, STATE), 0) < HEAD_DIM
                fresh += jnp.where(upper, total[0:1], total[1:2]) * enter[aligned(p, PAIR)]
            leave[aligned(p, PAIR)] = fresh.astype(leave.dtype)

        each(pairs, state_step)
        carry.start()

    arrive(3)
    conv_into(cconv, cbuf, tc, rows, STATE)
    scores = [
        lax.dot_general(cconv[span], bconv[0:reach], NT, preferred_element_type=jnp.float32)
        for span, reach, _ in bands
    ]

    def inner_step(p):
        x_pair = xconv[:, aligned(p, PAIR)]
        x_wide = x_pair.astype(jnp.float32)
        first = me * per_group + 2 * p
        direct = jnp.where(first_half, skip[first], skip[first + 1]) * x_wide
        x_mine = [
            jnp.where(mine, x_wide, 0.0).astype(jnp.bfloat16)
            for mine in (first_half, jnp.logical_not(first_half))
        ]
        for score, (span, reach, _) in zip(scores, bands):
            total = direct[span]
            for k in range(2):
                mixing = (score * decay[2 * p + k, span, 0:reach]).astype(jnp.bfloat16)
                total += jnp.dot(mixing, x_mine[k][0:reach], preferred_element_type=jnp.float32)
            acc[span, aligned(p, PAIR)] = total

    each(pairs, inner_step)

    if blocks == 2:

        @pl.when(has_prev)
        def _():
            carry.wait_recv()

    returns = {
        d: pltpu.make_async_remote_copy(
            src_ref=outgoing.at[d - 1],
            dst_ref=ret.at[me],
            send_sem=ret_send.at[d - 1],
            recv_sem=ret_recv.at[d - 1],
            device_id=at(base + partner(d)),
        )
        for d in (3, 2, 1)
    }

    def finish(with_outer):
        for d in (3, 2, 1, 0):
            here = pl.ds(pl.multiple_of(partner(d) * rows, rows), rows)
            result = acc[here]
            if with_outer:
                result += escale[here] * lax.dot_general(
                    cconv[here], enter[...].astype(jnp.bfloat16), NT,
                    preferred_element_type=jnp.float32,
                )
            if d == 0:
                ret[me] = result.astype(jnp.bfloat16)
            else:
                outgoing[d - 1] = result.astype(jnp.bfloat16)
                returns[d].start()

    @pl.when(has_prev)
    def _():
        finish(True)

    @pl.when(jnp.logical_not(has_prev))
    def _():
        finish(False)

    for d in (0, 1, 2, 3):
        if d > 0:
            returns[d].wait_recv()
        group = partner(d)
        lanes = aligned(group, width)
        gated = ret[group].astype(jnp.float32) * gate[:, lanes]
        mean_square = jnp.sum(gated * gated, axis=-1, keepdims=True) * (1.0 / width)
        out_ref[:, lanes] = (gated * lax.rsqrt(mean_square + eps) * gain[:, lanes]).astype(
            jnp.bfloat16
        )

    for n in range(4):
        for d in (1, 2, 3):
            sends[n, d].wait_send()

    @pl.when(sends_halo)
    def _():
        for member in range(members):
            halo(member).wait_send()

    @pl.when(has_next)
    def _():
        carry.wait_send()

    for d in (1, 2, 3):
        returns[d].wait_send()


def body(x_in, b_in, c_in, z_in, dt_raw, dt_bias, a_log, d_skip, conv_x, conv_b, conv_c, norm_gain):
    rows, channels = x_in.shape
    heads_here = dt_raw.shape[1]
    groups_here = b_in.shape[1] // STATE
    per_group = heads_here // groups_here
    members = BLOCK // rows
    blocks = lax.axis_size("seq") // members
    assert members == 4 and groups_here == members and per_group % 2 == 0
    width = per_group * HEAD_DIM
    pairs = per_group // 2
    tiles = halo_tiles(width)
    taps = conv_x.shape[0]
    carried = jnp.bfloat16 if blocks == 2 else jnp.float32
    low, full = jnp.bfloat16, jnp.float32
    dma = pltpu.SemaphoreType.DMA
    hbm = pl.BlockSpec(memory_space=pltpu.HBM)
    operands = [
        pltpu.with_memory_space_constraint(value, pltpu.HBM)
        for value in (
            x_in, b_in, c_in, z_in, dt_raw.T, dt_bias, a_log, d_skip,
            conv_x, conv_b, conv_c, norm_gain.reshape(1, channels),
        )
    ]
    return pl.pallas_call(
        functools.partial(kernel, blocks, members, rows, per_group, 1e-5),
        out_shape=jax.ShapeDtypeStruct((rows, channels), jnp.bfloat16),
        in_specs=[hbm] * 12,
        out_specs=pl.BlockSpec(memory_space=pltpu.VMEM),
        scratch_shapes=[
            pltpu.VMEM((LEAD + BLOCK, width), low),
            pltpu.VMEM((LEAD + BLOCK, STATE), low),
            pltpu.VMEM((LEAD + BLOCK, STATE), low),
            pltpu.VMEM((members, heads_here, rows), low),
            pltpu.VMEM((rows, channels), low),
            pltpu.VMEM((taps, width), low),
            pltpu.VMEM((taps, STATE), low),
            pltpu.VMEM((taps, STATE), low),
            pltpu.VMEM((1, channels), full),
            pltpu.SMEM((heads_here,), full),
            pltpu.SMEM((heads_here,), full),
            pltpu.SMEM((heads_here,), full),
            pltpu.VMEM((LEAD, channels), low),
            pltpu.VMEM((LEAD, b_in.shape[1]), low),
            pltpu.VMEM((LEAD, b_in.shape[1]), low),
            pltpu.VMEM((members, tiles * LEAD, 128), low),
            pltpu.VMEM((tiles * LEAD, 128), low),
            pltpu.VMEM((rows, channels), full),
            pltpu.VMEM((BLOCK, width), low),
            pltpu.VMEM((BLOCK, STATE), low),
            pltpu.VMEM((BLOCK, STATE), low),
            pltpu.VMEM((pairs, 16, BLOCK), full),
            pltpu.VMEM((pairs, BLOCK, 24), full),
            pltpu.VMEM((BLOCK, width), full),
            pltpu.VMEM((BLOCK, width), full),
            pltpu.VMEM((per_group, BLOCK, BLOCK), full),
            pltpu.VMEM((width, STATE), carried),
            pltpu.VMEM((width, STATE), carried),
            pltpu.VMEM((members - 1, rows, width), low),
            pltpu.VMEM((members, rows, width), low),
            dma((15,)),
            dma((4, 3)),
            dma((4, 3)),
            dma((members,)),
            dma,
            dma,
            dma,
            dma((3,)),
            dma((3,)),
        ],
        compiler_params=pltpu.CompilerParams(
            collective_id=0, has_side_effects=True, vmem_limit_bytes=32 * 1024 * 1024
        ),
    )(
        *operands,
    )


def solution(mesh):
    placed = (
        P(("rep", "seq"), "head"),
        P(("rep", "seq"), "head"),
        P(("rep", "seq"), "head"),
        P(("rep", "seq"), "head"),
        P(("rep", "seq"), "head"),
        P("head"),
        P("head"),
        P("head"),
        P(None, "head"),
        P(None, "head"),
        P(None, "head"),
        P("head"),
    )
    return jax.shard_map(
        body, mesh=mesh, in_specs=placed, out_specs=P(("rep", "seq"), "head"), check_vma=False
    )
```

```python
import functools

import jax
import jax.numpy as jnp
from jax import lax
from jax.experimental import pallas as pl
from jax.experimental.pallas import tpu as pltpu
from jax.sharding import PartitionSpec as P

HEAD_DIM = 64
STATE = 256
BLOCK = 256
LEAD = 16
PAIR = 2 * HEAD_DIM
NT = (((1,), (1,)), ((), ()))
TN = (((0,), (0,)), ((), ()))


def each(count, step):
    if count == 1:
        step(0)
    else:
        lax.fori_loop(0, count, lambda i, c: (step(i), c)[1], 0)


def aligned(index, unit):
    return pl.ds(pl.multiple_of(index * unit, unit), unit)


def silu(value):
    half = 0.5 * value
    return half * jnp.tanh(half) + half


def halo_spots(width):
    return [(n, k) for n, w in enumerate((width, STATE, STATE)) for k in range(0, w, 128)]


def halo_tiles(width):
    return -(-len(halo_spots(width)) // 5)


def conv_into(out_ref, buf_ref, taps_ref, rows, width):
    chunks = width // 128

    def lanes_step(k):
        lanes = aligned(k, 128)
        taps = taps_ref[:, lanes].astype(jnp.float32)
        count = taps.shape[0]
        for r in range(BLOCK // rows):
            part = buf_ref[r * rows : r * rows + rows + LEAD, lanes].astype(jnp.float32)
            total = taps[count - 1 : count] * part[LEAD:]
            for i in range(count - 1):
                total += taps[i : i + 1] * pltpu.roll(part, count - 1 - i, 0)[LEAD:]
            out_ref[r * rows : (r + 1) * rows, lanes] = silu(total).astype(jnp.bfloat16)

    if chunks <= 2:
        for k in range(chunks):
            lanes_step(k)
    else:
        each(chunks, lanes_step)


def kernel(
    blocks, members, rows, per_group, eps,
    x_hbm, b_hbm, c_hbm, z_hbm, dt_hbm, bias_hbm, alog_hbm, skip_hbm, tx_hbm, tb_hbm, tc_hbm, gain_hbm,
    out_ref,
    xbuf, bbuf, cbuf, dtbuf, zbuf, tx, tb, tc, gain, bias, alog, skip,
    xtail, btail, ctail, packed, unpacked, gate,
    xconv, bconv, cconv, rowbuf, colbuf, acc, escale, decay, enter, leave, outgoing, ret,
    local_sem, send_sem, recv_sem, halo_send, halo_recv, state_send, state_recv, ret_send, ret_recv,
):
    place = lax.axis_index("seq")
    me = lax.rem(place, members)
    block = place // members
    base = block * members
    width = per_group * HEAD_DIM
    pairs = per_group // 2
    high, low = me // 2, lax.rem(me, 2)

    def partner(d):
        return lax.rem(high + d // 2, 2) * 2 + lax.rem(low + d % 2, 2)

    def at(index):
        return {"seq": index}

    has_next = block < blocks - 1
    has_prev = block > 0
    is_last = me == members - 1

    barrier = pltpu.get_barrier_semaphore()
    for d in range(1, members):
        pl.semaphore_signal(barrier, inc=1, device_id=at(base + partner(d)))

    @pl.when(has_prev)
    def _():
        pl.semaphore_signal(barrier, inc=1, device_id=at(base - 1))

    @pl.when(jnp.logical_and(has_prev, jnp.logical_not(is_last)))
    def _():
        pl.semaphore_signal(barrier, inc=1, device_id=at(place - members))

    sources = (dt_hbm, x_hbm, b_hbm, c_hbm)
    buffers = (dtbuf, xbuf, bbuf, cbuf)
    widths = (None, width, STATE, STATE)

    def piece(n, group):
        if widths[n] is None:
            return sources[n]
        return sources[n].at[:, aligned(group, widths[n])]

    def slot(n, member):
        if widths[n] is None:
            return buffers[n].at[member]
        return buffers[n].at[pl.ds(pl.multiple_of(member * rows + LEAD, LEAD), rows)]

    own = [pltpu.make_async_copy(piece(n, me), slot(n, me), local_sem.at[n]) for n in range(4)]
    small = [
        pltpu.make_async_copy(tx_hbm.at[:, aligned(me, width)], tx, local_sem.at[4]),
        pltpu.make_async_copy(tb_hbm.at[:, aligned(me, STATE)], tb, local_sem.at[5]),
        pltpu.make_async_copy(tc_hbm.at[:, aligned(me, STATE)], tc, local_sem.at[6]),
        pltpu.make_async_copy(gain_hbm, gain, local_sem.at[7]),
        pltpu.make_async_copy(z_hbm, zbuf, local_sem.at[8]),
        pltpu.make_async_copy(bias_hbm, bias, local_sem.at[9]),
        pltpu.make_async_copy(alog_hbm, alog, local_sem.at[10]),
        pltpu.make_async_copy(skip_hbm, skip, local_sem.at[11]),
    ]
    tails = [
        pltpu.make_async_copy(hbm.at[rows - LEAD : rows], tail, local_sem.at[12 + k])
        for k, (hbm, tail) in enumerate(((x_hbm, xtail), (b_hbm, btail), (c_hbm, ctail)))
    ]
    sends_halo = jnp.logical_and(has_next, is_last)

    @pl.when(sends_halo)
    def _():
        for copy in tails:
            copy.start()

    for copy in own + small:
        copy.start()

    @pl.when(jnp.logical_not(has_prev))
    def _():
        for buf in (xbuf, bbuf, cbuf):
            buf[0:LEAD] = jnp.zeros((LEAD, buf.shape[1]), jnp.bfloat16)
        enter[...] = jnp.zeros_like(enter)

    next_count = jnp.where(is_last, members, 1)
    pl.semaphore_wait(barrier, members - 1 + jnp.where(has_next, next_count, 0))

    sends = {}
    for n in range(4):
        for d in (3, 2, 1):
            sends[n, d] = pltpu.make_async_remote_copy(
                src_ref=piece(n, partner(d)),
                dst_ref=slot(n, me),
                send_sem=send_sem.at[n, d - 1],
                recv_sem=recv_sem.at[n, d - 1],
                device_id=at(base + partner(d)),
            )

    def halo(member):
        return pltpu.make_async_remote_copy(
            src_ref=packed.at[member],
            dst_ref=unpacked,
            send_sem=halo_send.at[member],
            recv_sem=halo_recv,
            device_id=at(base + members + member),
        )

    def start(n):
        for d in (3, 2, 1):
            sends[n, d].start()

    for n in range(3):
        start(n)

    yields = lax.axis_index("head") > 0

    @pl.when(jnp.logical_not(yields))
    def _():
        start(3)

    spots = halo_spots(width)
    inside = lax.broadcasted_iota(jnp.int32, (LEAD, 128), 0)

    @pl.when(sends_halo)
    def _():
        for copy in tails:
            copy.wait()
        for member in range(members):
            tile = jnp.zeros((LEAD, 128), jnp.float32)
            for q, (n, start) in enumerate(spots):
                place_in = 3 * (q % 5)
                tail = (xtail, btail, ctail)[n]
                offset = member * (width if n == 0 else STATE) + start
                part = tail[:, offset : offset + 128].astype(jnp.float32)
                part = pltpu.roll(part, (place_in + 3) % LEAD, 0)
                fits = jnp.logical_and(inside >= place_in, inside < place_in + 3)
                tile = jnp.where(fits, part, tile)
                if q % 5 == 4 or q == len(spots) - 1:
                    first = q // 5 * LEAD
                    packed[member, first : first + LEAD] = tile.astype(jnp.bfloat16)
            halo(member).start()

    def take_halo():
        @pl.when(has_prev)
        def _():
            halo(0).wait_recv()
            for q, (n, start) in enumerate(spots):
                first = q // 5 * LEAD
                tile = unpacked[first : first + LEAD].astype(jnp.float32)
                part = pltpu.roll(tile, (13 - 3 * (q % 5)) % LEAD, 0)
                buffers[n + 1][0:LEAD, start : start + 128] = part.astype(jnp.bfloat16)

    def arrive(n):
        own[n].wait()
        for d in (1, 2, 3):
            sends[n, d].wait_recv()

    arrive(0)
    raw = jnp.concatenate([dtbuf[m] for m in range(members)], axis=1).astype(jnp.float32)
    for copy in small[5:]:
        copy.wait()
    heads_here = raw.shape[0]
    head_id = lax.broadcasted_iota(jnp.int32, (heads_here, BLOCK), 0)
    sub = lax.broadcasted_iota(jnp.int32, (8, BLOCK), 0)
    up_to = (
        lax.broadcasted_iota(jnp.int32, (BLOCK, BLOCK), 0)
        <= lax.broadcasted_iota(jnp.int32, (BLOCK, BLOCK), 1)
    ).astype(jnp.float32).astype(jnp.bfloat16)

    def rates_step(p):
        first = me * per_group + 2 * p

        def row(k):
            return jnp.sum(jnp.where(head_id == first + k, raw, 0.0), axis=0, keepdims=True)

        def both(ref):
            return jnp.where(sub == 0, ref[first], ref[first + 1])

        v = jnp.where(sub == 0, row(0), row(1)) + both(bias)
        rates = jnp.maximum(v, 0.0) + jnp.log1p(jnp.exp(-jnp.abs(v)))
        decays = rates * -jnp.exp(both(alog))
        top = decays.astype(jnp.bfloat16).astype(jnp.float32)
        rest = decays - top
        middle = rest.astype(jnp.bfloat16).astype(jnp.float32)
        stacked = jnp.concatenate([top, middle, rest - middle, jnp.zeros_like(top)], axis=0)
        summed = jnp.dot(stacked.astype(jnp.bfloat16), up_to, preferred_element_type=jnp.float32)
        log_decay = summed[0:8] + summed[8:16] + summed[16:24]
        weight = jnp.exp(log_decay[:, BLOCK - 1 : BLOCK] - log_decay) * rates
        rowbuf[p, 0:8] = log_decay
        rowbuf[p, 8:16] = rates
        colbuf[p] = jnp.transpose(
            jnp.concatenate([log_decay, weight, jnp.exp(log_decay)], axis=0)
        )

    half = BLOCK // 2
    bands = []
    for r in range(2):
        span, reach = slice(r * half, (r + 1) * half), (r + 1) * half
        causal = lax.broadcasted_iota(jnp.int32, (half, reach), 0) + r * half >= (
            lax.broadcasted_iota(jnp.int32, (half, reach), 1)
        )
        bands.append((span, reach, causal))

    first_half = lax.broadcasted_iota(jnp.int32, (BLOCK, PAIR), 1) < HEAD_DIM

    def spread(p, column):
        return jnp.where(
            first_half, colbuf[p, :, column : column + 1], colbuf[p, :, column + 1 : column + 2]
        )

    def decay_step(p):
        for span, reach, causal in bands:
            for k in range(2):
                gap = colbuf[p, span, k : k + 1] - rowbuf[p, k : k + 1, 0:reach]
                decay[2 * p + k, span, 0:reach] = jnp.where(
                    causal,
                    jnp.exp(jnp.where(causal, gap, 0.0)) * rowbuf[p, 8 + k : 9 + k, 0:reach],
                    0.0,
                )
        escale[:, aligned(p, PAIR)] = spread(p, 16)

    each(pairs, rates_step)
    each(pairs, decay_step)
    for copy in small[3:5]:
        copy.wait()
    for group in range(members):
        lanes = slice(group * width, (group + 1) * width)
        gate[:, lanes] = silu(zbuf[:, lanes].astype(jnp.float32))

    for copy in small[:3]:
        copy.wait()
    take_halo()
    arrive(1)
    conv_into(xconv, xbuf, tx, rows, width)
    arrive(2)

    @pl.when(yields)
    def _():
        start(3)

    conv_into(bconv, bbuf, tb, rows, STATE)

    carry = pltpu.make_async_remote_copy(
        src_ref=leave,
        dst_ref=enter,
        send_sem=state_send,
        recv_sem=state_recv,
        device_id=at(place + members),
    )

    if blocks > 2:

        @pl.when(has_prev)
        def _():
            carry.wait_recv()

    @pl.when(has_next)
    def _():
        def state_step(p):
            scaled = (xconv[:, aligned(p, PAIR)].astype(jnp.float32) * spread(p, 8)).astype(
                jnp.bfloat16
            )
            fresh = lax.dot_general(scaled, bconv[...], TN, preferred_element_type=jnp.float32)
            if blocks > 2:
                total = jnp.exp(rowbuf[p, 0:8, BLOCK - 1 : BLOCK])
                upper = lax.broadcasted_iota(jnp.int32, (PAIR, STATE), 0) < HEAD_DIM
                fresh += jnp.where(upper, total[0:1], total[1:2]) * enter[aligned(p, PAIR)]
            leave[aligned(p, PAIR)] = fresh.astype(leave.dtype)

        each(pairs, state_step)
        carry.start()

    arrive(3)
    conv_into(cconv, cbuf, tc, rows, STATE)
    scores = [
        lax.dot_general(cconv[span], bconv[0:reach], NT, preferred_element_type=jnp.float32)
        for span, reach, _ in bands
    ]

    def inner_step(p):
        x_pair = xconv[:, aligned(p, PAIR)]
        x_wide = x_pair.astype(jnp.float32)
        first = me * per_group + 2 * p
        direct = jnp.where(first_half, skip[first], skip[first + 1]) * x_wide
        x_mine = [
            jnp.where(mine, x_wide, 0.0).astype(jnp.bfloat16)
            for mine in (first_half, jnp.logical_not(first_half))
        ]
        for score, (span, reach, _) in zip(scores, bands):
            total = direct[span]
            for k in range(2):
                mixing = (score * decay[2 * p + k, span, 0:reach]).astype(jnp.bfloat16)
                total += jnp.dot(mixing, x_mine[k][0:reach], preferred_element_type=jnp.float32)
            acc[span, aligned(p, PAIR)] = total

    each(pairs, inner_step)

    if blocks == 2:

        @pl.when(has_prev)
        def _():
            carry.wait_recv()

    returns = {
        d: pltpu.make_async_remote_copy(
            src_ref=outgoing.at[d - 1],
            dst_ref=ret.at[me],
            send_sem=ret_send.at[d - 1],
            recv_sem=ret_recv.at[d - 1],
            device_id=at(base + partner(d)),
        )
        for d in (3, 2, 1)
    }

    def finish(with_outer):
        for d in (3, 2, 1, 0):
            here = pl.ds(pl.multiple_of(partner(d) * rows, rows), rows)
            result = acc[here]
            if with_outer:
                result += escale[here] * lax.dot_general(
                    cconv[here], enter[...].astype(jnp.bfloat16), NT,
                    preferred_element_type=jnp.float32,
                )
            if d == 0:
                ret[me] = result.astype(jnp.bfloat16)
            else:
                outgoing[d - 1] = result.astype(jnp.bfloat16)
                returns[d].start()

    @pl.when(has_prev)
    def _():
        finish(True)

    @pl.when(jnp.logical_not(has_prev))
    def _():
        finish(False)

    for d in (0, 1, 2, 3):
        if d > 0:
            returns[d].wait_recv()
        group = partner(d)
        lanes = aligned(group, width)
        gated = ret[group].astype(jnp.float32) * gate[:, lanes]
        mean_square = jnp.sum(gated * gated, axis=-1, keepdims=True) * (1.0 / width)
        out_ref[:, lanes] = (gated * lax.rsqrt(mean_square + eps) * gain[:, lanes]).astype(
            jnp.bfloat16
        )

    for n in range(4):
        for d in (1, 2, 3):
            sends[n, d].wait_send()

    @pl.when(sends_halo)
    def _():
        for member in range(members):
            halo(member).wait_send()

    @pl.when(has_next)
    def _():
        carry.wait_send()

    for d in (1, 2, 3):
        returns[d].wait_send()


def body(x_in, b_in, c_in, z_in, dt_raw, dt_bias, a_log, d_skip, conv_x, conv_b, conv_c, norm_gain):
    rows, channels = x_in.shape
    heads_here = dt_raw.shape[1]
    groups_here = b_in.shape[1] // STATE
    per_group = heads_here // groups_here
    members = BLOCK // rows
    blocks = lax.axis_size("seq") // members
    assert members == 4 and groups_here == members and per_group % 2 == 0
    width = per_group * HEAD_DIM
    pairs = per_group // 2
    tiles = halo_tiles(width)
    taps = conv_x.shape[0]
    carried = jnp.bfloat16 if blocks == 2 else jnp.float32
    low, full = jnp.bfloat16, jnp.float32
    dma = pltpu.SemaphoreType.DMA
    hbm = pl.BlockSpec(memory_space=pltpu.HBM)
    operands = [
        pltpu.with_memory_space_constraint(value, pltpu.HBM)
        for value in (
            x_in, b_in, c_in, z_in, dt_raw.T, dt_bias, a_log, d_skip,
            conv_x, conv_b, conv_c, norm_gain.reshape(1, channels),
        )
    ]
    return pl.pallas_call(
        functools.partial(kernel, blocks, members, rows, per_group, 1e-5),
        out_shape=jax.ShapeDtypeStruct((rows, channels), jnp.bfloat16),
        in_specs=[hbm] * 12,
        out_specs=pl.BlockSpec(memory_space=pltpu.VMEM),
        scratch_shapes=[
            pltpu.VMEM((LEAD + BLOCK, width), low),
            pltpu.VMEM((LEAD + BLOCK, STATE), low),
            pltpu.VMEM((LEAD + BLOCK, STATE), low),
            pltpu.VMEM((members, heads_here, rows), low),
            pltpu.VMEM((rows, channels), low),
            pltpu.VMEM((taps, width), low),
            pltpu.VMEM((taps, STATE), low),
            pltpu.VMEM((taps, STATE), low),
            pltpu.VMEM((1, channels), full),
            pltpu.SMEM((heads_here,), full),
            pltpu.SMEM((heads_here,), full),
            pltpu.SMEM((heads_here,), full),
            pltpu.VMEM((LEAD, channels), low),
            pltpu.VMEM((LEAD, b_in.shape[1]), low),
            pltpu.VMEM((LEAD, b_in.shape[1]), low),
            pltpu.VMEM((members, tiles * LEAD, 128), low),
            pltpu.VMEM((tiles * LEAD, 128), low),
            pltpu.VMEM((rows, channels), full),
            pltpu.VMEM((BLOCK, width), low),
            pltpu.VMEM((BLOCK, STATE), low),
            pltpu.VMEM((BLOCK, STATE), low),
            pltpu.VMEM((pairs, 16, BLOCK), full),
            pltpu.VMEM((pairs, BLOCK, 24), full),
            pltpu.VMEM((BLOCK, width), full),
            pltpu.VMEM((BLOCK, width), full),
            pltpu.VMEM((per_group, BLOCK, BLOCK), full),
            pltpu.VMEM((width, STATE), carried),
            pltpu.VMEM((width, STATE), carried),
            pltpu.VMEM((members - 1, rows, width), low),
            pltpu.VMEM((members, rows, width), low),
            dma((15,)),
            dma((4, 3)),
            dma((4, 3)),
            dma((members,)),
            dma,
            dma,
            dma,
            dma((3,)),
            dma((3,)),
        ],
        compiler_params=pltpu.CompilerParams(
            collective_id=0, has_side_effects=True, vmem_limit_bytes=32 * 1024 * 1024
        ),
    )(
        *operands,
    )


def solution(mesh):
    placed = (
        P(("rep", "seq"), "head"),
        P(("rep", "seq"), "head"),
        P(("rep", "seq"), "head"),
        P(("rep", "seq"), "head"),
        P(("rep", "seq"), "head"),
        P("head"),
        P("head"),
        P("head"),
        P(None, "head"),
        P(None, "head"),
        P(None, "head"),
        P("head"),
    )
    return jax.shard_map(
        body, mesh=mesh, in_specs=placed, out_specs=P(("rep", "seq"), "head"), check_vma=False
    )
```

```python
import functools

import jax
import jax.numpy as jnp
from jax import lax
from jax.experimental import pallas as pl
from jax.experimental.pallas import tpu as pltpu
from jax.sharding import PartitionSpec as P

HEAD_DIM = 64
STATE = 256
BLOCK = 256
LEAD = 16
PAIR = 2 * HEAD_DIM
NT = (((1,), (1,)), ((), ()))
TN = (((0,), (0,)), ((), ()))


def each(count, step):
    if count == 1:
        step(0)
    else:
        lax.fori_loop(0, count, lambda i, c: (step(i), c)[1], 0)


def aligned(index, unit):
    return pl.ds(pl.multiple_of(index * unit, unit), unit)


def silu(value):
    half = 0.5 * value
    return half * jnp.tanh(half) + half


def halo_spots(width):
    return [(n, k) for n, w in enumerate((width, STATE, STATE)) for k in range(0, w, 128)]


def halo_tiles(width):
    return -(-len(halo_spots(width)) // 5)


def conv_into(out_ref, buf_ref, taps_ref, rows, width, only=None):
    chunks = width // 128

    def lanes_step(k):
        lanes = aligned(k, 128)
        taps = taps_ref[:, lanes].astype(jnp.float32)
        count = taps.shape[0]
        for r in range(BLOCK // rows):
            part = buf_ref[r * rows : r * rows + rows + LEAD, lanes].astype(jnp.float32)
            total = taps[count - 1 : count] * part[LEAD:]
            for i in range(count - 1):
                total += taps[i : i + 1] * pltpu.roll(part, count - 1 - i, 0)[LEAD:]
            out_ref[r * rows : (r + 1) * rows, lanes] = silu(total).astype(jnp.bfloat16)

    if only is not None:
        lanes_step(only)
    elif chunks <= 2:
        for k in range(chunks):
            lanes_step(k)
    else:
        each(chunks, lanes_step)


def kernel(
    blocks, members, rows, per_group, eps,
    x_hbm, b_hbm, c_hbm, z_hbm, dt_hbm, bias_hbm, alog_hbm, skip_hbm, tx_hbm, tb_hbm, tc_hbm, gain_hbm,
    out_ref,
    xbuf, bbuf, cbuf, dtbuf, zbuf, tx, tb, tc, gain, bias, alog, skip,
    xtail, btail, ctail, packed, unpacked, gate,
    xconv, bconv, cconv, rowbuf, colbuf, acc, escale, decay, scaled, enter, leave, outgoing, ret,
    local_sem, send_sem, recv_sem, halo_send, halo_recv, state_send, state_recv, ret_send, ret_recv,
):
    place = lax.axis_index("seq")
    me = lax.rem(place, members)
    block = place // members
    base = block * members
    width = per_group * HEAD_DIM
    pairs = per_group // 2
    high, low = me // 2, lax.rem(me, 2)

    def partner(d):
        return lax.rem(high + d // 2, 2) * 2 + lax.rem(low + d % 2, 2)

    def at(index):
        return {"seq": index}

    has_next = block < blocks - 1
    has_prev = block > 0
    is_last = me == members - 1

    barrier = pltpu.get_barrier_semaphore()
    for d in range(1, members):
        pl.semaphore_signal(barrier, inc=1, device_id=at(base + partner(d)))

    @pl.when(has_prev)
    def _():
        pl.semaphore_signal(barrier, inc=1, device_id=at(base - 1))

    @pl.when(jnp.logical_and(has_prev, jnp.logical_not(is_last)))
    def _():
        pl.semaphore_signal(barrier, inc=1, device_id=at(place - members))

    sources = (dt_hbm, x_hbm, b_hbm, c_hbm)
    buffers = (dtbuf, xbuf, bbuf, cbuf)
    widths = (None, width, STATE, STATE)

    def piece(n, group):
        if widths[n] is None:
            return sources[n]
        return sources[n].at[:, aligned(group, widths[n])]

    def slot(n, member):
        if widths[n] is None:
            return buffers[n].at[member]
        return buffers[n].at[pl.ds(pl.multiple_of(member * rows + LEAD, LEAD), rows)]

    own = [pltpu.make_async_copy(piece(n, me), slot(n, me), local_sem.at[n]) for n in range(4)]
    small = [
        pltpu.make_async_copy(tx_hbm.at[:, aligned(me, width)], tx, local_sem.at[4]),
        pltpu.make_async_copy(tb_hbm.at[:, aligned(me, STATE)], tb, local_sem.at[5]),
        pltpu.make_async_copy(tc_hbm.at[:, aligned(me, STATE)], tc, local_sem.at[6]),
        pltpu.make_async_copy(gain_hbm, gain, local_sem.at[7]),
        pltpu.make_async_copy(z_hbm, zbuf, local_sem.at[8]),
        pltpu.make_async_copy(bias_hbm, bias, local_sem.at[9]),
        pltpu.make_async_copy(alog_hbm, alog, local_sem.at[10]),
        pltpu.make_async_copy(skip_hbm, skip, local_sem.at[11]),
    ]
    tails = [
        pltpu.make_async_copy(hbm.at[rows - LEAD : rows], tail, local_sem.at[12 + k])
        for k, (hbm, tail) in enumerate(((x_hbm, xtail), (b_hbm, btail), (c_hbm, ctail)))
    ]
    sends_halo = jnp.logical_and(has_next, is_last)

    @pl.when(sends_halo)
    def _():
        for copy in tails:
            copy.start()

    for copy in own + small:
        copy.start()

    @pl.when(jnp.logical_not(has_prev))
    def _():
        for buf in (xbuf, bbuf, cbuf):
            buf[0:LEAD] = jnp.zeros((LEAD, buf.shape[1]), jnp.bfloat16)
        enter[...] = jnp.zeros_like(enter)

    next_count = jnp.where(is_last, members, 1)
    pl.semaphore_wait(barrier, members - 1 + jnp.where(has_next, next_count, 0))

    sends = {}
    for n in range(4):
        for d in (3, 2, 1):
            sends[n, d] = pltpu.make_async_remote_copy(
                src_ref=piece(n, partner(d)),
                dst_ref=slot(n, me),
                send_sem=send_sem.at[n, d - 1],
                recv_sem=recv_sem.at[n, d - 1],
                device_id=at(base + partner(d)),
            )

    def halo(member):
        return pltpu.make_async_remote_copy(
            src_ref=packed.at[member],
            dst_ref=unpacked,
            send_sem=halo_send.at[member],
            recv_sem=halo_recv,
            device_id=at(base + members + member),
        )

    def start(n):
        for d in (3, 2, 1):
            sends[n, d].start()

    for n in range(3):
        start(n)

    yields = lax.axis_index("head") > 0

    @pl.when(jnp.logical_not(yields))
    def _():
        start(3)

    spots = halo_spots(width)
    inside = lax.broadcasted_iota(jnp.int32, (LEAD, 128), 0)

    @pl.when(sends_halo)
    def _():
        for copy in tails:
            copy.wait()
        for member in range(members):
            tile = jnp.zeros((LEAD, 128), jnp.float32)
            for q, (n, start) in enumerate(spots):
                place_in = 3 * (q % 5)
                tail = (xtail, btail, ctail)[n]
                offset = member * (width if n == 0 else STATE) + start
                part = tail[:, offset : offset + 128].astype(jnp.float32)
                part = pltpu.roll(part, (place_in + 3) % LEAD, 0)
                fits = jnp.logical_and(inside >= place_in, inside < place_in + 3)
                tile = jnp.where(fits, part, tile)
                if q % 5 == 4 or q == len(spots) - 1:
                    first = q // 5 * LEAD
                    packed[member, first : first + LEAD] = tile.astype(jnp.bfloat16)
            halo(member).start()

    def take_halo():
        @pl.when(has_prev)
        def _():
            halo(0).wait_recv()
            for q, (n, start) in enumerate(spots):
                first = q // 5 * LEAD
                tile = unpacked[first : first + LEAD].astype(jnp.float32)
                part = pltpu.roll(tile, (13 - 3 * (q % 5)) % LEAD, 0)
                buffers[n + 1][0:LEAD, start : start + 128] = part.astype(jnp.bfloat16)

    def arrive(n):
        own[n].wait()
        for d in (1, 2, 3):
            sends[n, d].wait_recv()

    arrive(0)
    raw = jnp.concatenate([dtbuf[m] for m in range(members)], axis=1).astype(jnp.float32)
    for copy in small[5:]:
        copy.wait()
    heads_here = raw.shape[0]
    head_id = lax.broadcasted_iota(jnp.int32, (heads_here, BLOCK), 0)
    sub = lax.broadcasted_iota(jnp.int32, (8, BLOCK), 0)
    up_to = (
        lax.broadcasted_iota(jnp.int32, (BLOCK, BLOCK), 0)
        <= lax.broadcasted_iota(jnp.int32, (BLOCK, BLOCK), 1)
    ).astype(jnp.float32).astype(jnp.bfloat16)

    def rates_step(p):
        first = me * per_group + 2 * p

        def row(k):
            return jnp.sum(jnp.where(head_id == first + k, raw, 0.0), axis=0, keepdims=True)

        def both(ref):
            return jnp.where(sub == 0, ref[first], ref[first + 1])

        v = jnp.where(sub == 0, row(0), row(1)) + both(bias)
        rates = jnp.maximum(v, 0.0) + jnp.log1p(jnp.exp(-jnp.abs(v)))
        decays = rates * -jnp.exp(both(alog))
        top = decays.astype(jnp.bfloat16).astype(jnp.float32)
        rest = decays - top
        middle = rest.astype(jnp.bfloat16).astype(jnp.float32)
        stacked = jnp.concatenate([top, middle, rest - middle, jnp.zeros_like(top)], axis=0)
        summed = jnp.dot(stacked.astype(jnp.bfloat16), up_to, preferred_element_type=jnp.float32)
        log_decay = summed[0:8] + summed[8:16] + summed[16:24]
        weight = jnp.exp(log_decay[:, BLOCK - 1 : BLOCK] - log_decay) * rates
        rowbuf[p, 0:8] = log_decay
        rowbuf[p, 8:16] = rates
        colbuf[p] = jnp.transpose(
            jnp.concatenate([log_decay, weight, jnp.exp(log_decay)], axis=0)
        )

    half = BLOCK // 2
    bands = []
    for r in range(2):
        span, reach = slice(r * half, (r + 1) * half), (r + 1) * half
        causal = lax.broadcasted_iota(jnp.int32, (half, reach), 0) + r * half >= (
            lax.broadcasted_iota(jnp.int32, (half, reach), 1)
        )
        bands.append((span, reach, causal))

    first_half = lax.broadcasted_iota(jnp.int32, (BLOCK, PAIR), 1) < HEAD_DIM

    def spread(p, column):
        return jnp.where(
            first_half, colbuf[p, :, column : column + 1], colbuf[p, :, column + 1 : column + 2]
        )

    def decay_step(p):
        for span, reach, causal in bands:
            for k in range(2):
                gap = colbuf[p, span, k : k + 1] - rowbuf[p, k : k + 1, 0:reach]
                decay[2 * p + k, span, 0:reach] = jnp.where(
                    causal,
                    jnp.exp(jnp.where(causal, gap, 0.0)) * rowbuf[p, 8 + k : 9 + k, 0:reach],
                    0.0,
                )
        escale[:, aligned(p, PAIR)] = spread(p, 16)

    each(pairs, rates_step)
    each(pairs, decay_step)
    for copy in small[3:5]:
        copy.wait()
    for group in range(members):
        lanes = slice(group * width, (group + 1) * width)
        gate[:, lanes] = silu(zbuf[:, lanes].astype(jnp.float32))

    for copy in small[:3]:
        copy.wait()
    take_halo()
    arrive(1)
    conv_into(xconv, xbuf, tx, rows, width)
    def scale_step(p):
        scaled[:, aligned(p, PAIR)] = (
            xconv[:, aligned(p, PAIR)].astype(jnp.float32) * spread(p, 8)
        ).astype(jnp.bfloat16)

    each(pairs, scale_step)
    arrive(2)

    @pl.when(yields)
    def _():
        start(3)

    halves = [slice(k * 128, (k + 1) * 128) for k in range(STATE // 128)]
    carries = [
        pltpu.make_async_remote_copy(
            src_ref=leave.at[:, lanes],
            dst_ref=enter.at[:, lanes],
            send_sem=state_send.at[k],
            recv_sem=state_recv.at[k],
            device_id=at(place + members),
        )
        for k, lanes in enumerate(halves)
    ]

    def take_states():
        @pl.when(has_prev)
        def _():
            for carry in carries:
                carry.wait_recv()

    if blocks > 2:
        take_states()

    for k, lanes in enumerate(halves):
        conv_into(bconv, bbuf, tb, rows, STATE, k)

        @pl.when(has_next)
        def _(k=k, lanes=lanes):
            def state_step(p):
                fresh = lax.dot_general(
                    scaled[:, aligned(p, PAIR)], bconv[:, lanes], TN,
                    preferred_element_type=jnp.float32,
                )
                if blocks > 2:
                    total = jnp.exp(rowbuf[p, 0:8, BLOCK - 1 : BLOCK])
                    upper = lax.broadcasted_iota(jnp.int32, (PAIR, 128), 0) < HEAD_DIM
                    fresh += jnp.where(upper, total[0:1], total[1:2]) * enter[aligned(p, PAIR), lanes]
                leave[aligned(p, PAIR), lanes] = fresh.astype(leave.dtype)

            each(pairs, state_step)
            carries[k].start()

    arrive(3)
    conv_into(cconv, cbuf, tc, rows, STATE)
    scores = [
        lax.dot_general(cconv[span], bconv[0:reach], NT, preferred_element_type=jnp.float32)
        for span, reach, _ in bands
    ]

    def inner_step(p):
        x_pair = xconv[:, aligned(p, PAIR)]
        x_wide = x_pair.astype(jnp.float32)
        first = me * per_group + 2 * p
        direct = jnp.where(first_half, skip[first], skip[first + 1]) * x_wide
        x_mine = [
            jnp.where(mine, x_wide, 0.0).astype(jnp.bfloat16)
            for mine in (first_half, jnp.logical_not(first_half))
        ]
        for score, (span, reach, _) in zip(scores, bands):
            total = direct[span]
            for k in range(2):
                mixing = (score * decay[2 * p + k, span, 0:reach]).astype(jnp.bfloat16)
                total += jnp.dot(mixing, x_mine[k][0:reach], preferred_element_type=jnp.float32)
            acc[span, aligned(p, PAIR)] = total

    each(pairs, inner_step)

    if blocks == 2:
        take_states()

    returns = {
        d: pltpu.make_async_remote_copy(
            src_ref=outgoing.at[d - 1],
            dst_ref=ret.at[me],
            send_sem=ret_send.at[d - 1],
            recv_sem=ret_recv.at[d - 1],
            device_id=at(base + partner(d)),
        )
        for d in (3, 2, 1)
    }

    def finish(with_outer):
        for d in (3, 2, 1, 0):
            here = pl.ds(pl.multiple_of(partner(d) * rows, rows), rows)
            result = acc[here]
            if with_outer:
                result += escale[here] * lax.dot_general(
                    cconv[here], enter[...].astype(jnp.bfloat16), NT,
                    preferred_element_type=jnp.float32,
                )
            if d == 0:
                ret[me] = result.astype(jnp.bfloat16)
            else:
                outgoing[d - 1] = result.astype(jnp.bfloat16)
                returns[d].start()

    @pl.when(has_prev)
    def _():
        finish(True)

    @pl.when(jnp.logical_not(has_prev))
    def _():
        finish(False)

    for d in (0, 1, 2, 3):
        if d > 0:
            returns[d].wait_recv()
        group = partner(d)
        lanes = aligned(group, width)
        gated = ret[group].astype(jnp.float32) * gate[:, lanes]
        mean_square = jnp.sum(gated * gated, axis=-1, keepdims=True) * (1.0 / width)
        out_ref[:, lanes] = (gated * lax.rsqrt(mean_square + eps) * gain[:, lanes]).astype(
            jnp.bfloat16
        )

    for n in range(4):
        for d in (1, 2, 3):
            sends[n, d].wait_send()

    @pl.when(sends_halo)
    def _():
        for member in range(members):
            halo(member).wait_send()

    @pl.when(has_next)
    def _():
        for carry in carries:
            carry.wait_send()

    for d in (1, 2, 3):
        returns[d].wait_send()


def body(x_in, b_in, c_in, z_in, dt_raw, dt_bias, a_log, d_skip, conv_x, conv_b, conv_c, norm_gain):
    rows, channels = x_in.shape
    heads_here = dt_raw.shape[1]
    groups_here = b_in.shape[1] // STATE
    per_group = heads_here // groups_here
    members = BLOCK // rows
    blocks = lax.axis_size("seq") // members
    assert members == 4 and groups_here == members and per_group % 2 == 0
    width = per_group * HEAD_DIM
    pairs = per_group // 2
    tiles = halo_tiles(width)
    taps = conv_x.shape[0]
    carried = jnp.bfloat16 if blocks == 2 else jnp.float32
    low, full = jnp.bfloat16, jnp.float32
    dma = pltpu.SemaphoreType.DMA
    hbm = pl.BlockSpec(memory_space=pltpu.HBM)
    operands = [
        pltpu.with_memory_space_constraint(value, pltpu.HBM)
        for value in (
            x_in, b_in, c_in, z_in, dt_raw.T, dt_bias, a_log, d_skip,
            conv_x, conv_b, conv_c, norm_gain.reshape(1, channels),
        )
    ]
    return pl.pallas_call(
        functools.partial(kernel, blocks, members, rows, per_group, 1e-5),
        out_shape=jax.ShapeDtypeStruct((rows, channels), jnp.bfloat16),
        in_specs=[hbm] * 12,
        out_specs=pl.BlockSpec(memory_space=pltpu.VMEM),
        scratch_shapes=[
            pltpu.VMEM((LEAD + BLOCK, width), low),
            pltpu.VMEM((LEAD + BLOCK, STATE), low),
            pltpu.VMEM((LEAD + BLOCK, STATE), low),
            pltpu.VMEM((members, heads_here, rows), low),
            pltpu.VMEM((rows, channels), low),
            pltpu.VMEM((taps, width), low),
            pltpu.VMEM((taps, STATE), low),
            pltpu.VMEM((taps, STATE), low),
            pltpu.VMEM((1, channels), full),
            pltpu.SMEM((heads_here,), full),
            pltpu.SMEM((heads_here,), full),
            pltpu.SMEM((heads_here,), full),
            pltpu.VMEM((LEAD, channels), low),
            pltpu.VMEM((LEAD, b_in.shape[1]), low),
            pltpu.VMEM((LEAD, b_in.shape[1]), low),
            pltpu.VMEM((members, tiles * LEAD, 128), low),
            pltpu.VMEM((tiles * LEAD, 128), low),
            pltpu.VMEM((rows, channels), full),
            pltpu.VMEM((BLOCK, width), low),
            pltpu.VMEM((BLOCK, STATE), low),
            pltpu.VMEM((BLOCK, STATE), low),
            pltpu.VMEM((pairs, 16, BLOCK), full),
            pltpu.VMEM((pairs, BLOCK, 24), full),
            pltpu.VMEM((BLOCK, width), full),
            pltpu.VMEM((BLOCK, width), full),
            pltpu.VMEM((per_group, BLOCK, BLOCK), full),
            pltpu.VMEM((BLOCK, width), low),
            pltpu.VMEM((width, STATE), carried),
            pltpu.VMEM((width, STATE), carried),
            pltpu.VMEM((members - 1, rows, width), low),
            pltpu.VMEM((members, rows, width), low),
            dma((15,)),
            dma((4, 3)),
            dma((4, 3)),
            dma((members,)),
            dma,
            dma((2,)),
            dma((2,)),
            dma((3,)),
            dma((3,)),
        ],
        compiler_params=pltpu.CompilerParams(
            collective_id=0, has_side_effects=True, vmem_limit_bytes=32 * 1024 * 1024
        ),
    )(
        *operands,
    )


def solution(mesh):
    placed = (
        P(("rep", "seq"), "head"),
        P(("rep", "seq"), "head"),
        P(("rep", "seq"), "head"),
        P(("rep", "seq"), "head"),
        P(("rep", "seq"), "head"),
        P("head"),
        P("head"),
        P("head"),
        P(None, "head"),
        P(None, "head"),
        P(None, "head"),
        P("head"),
    )
    return jax.shard_map(
        body, mesh=mesh, in_specs=placed, out_specs=P(("rep", "seq"), "head"), check_vma=False
    )
```

```python
import functools

import jax
import jax.numpy as jnp
from jax import lax
from jax.experimental import pallas as pl
from jax.experimental.pallas import tpu as pltpu
from jax.sharding import PartitionSpec as P

HEAD_DIM = 64
STATE = 256
BLOCK = 256
LEAD = 16
PAIR = 2 * HEAD_DIM
NT = (((1,), (1,)), ((), ()))
TN = (((0,), (0,)), ((), ()))


def each(count, step):
    if count == 1:
        step(0)
    else:
        lax.fori_loop(0, count, lambda i, c: (step(i), c)[1], 0)


def aligned(index, unit):
    return pl.ds(pl.multiple_of(index * unit, unit), unit)


def silu(value):
    half = 0.5 * value
    return half * jnp.tanh(half) + half


def halo_spots(width):
    return [(n, k) for n, w in enumerate((width, STATE, STATE)) for k in range(0, w, 128)]


def halo_tiles(width):
    return -(-len(halo_spots(width)) // 5)


def conv_into(out_ref, buf_ref, taps_ref, rows, width, only=None):
    chunks = width // 128

    def lanes_step(k):
        lanes = aligned(k, 128)
        taps = taps_ref[:, lanes].astype(jnp.float32)
        count = taps.shape[0]
        for r in range(BLOCK // rows):
            part = buf_ref[r * rows : r * rows + rows + LEAD, lanes].astype(jnp.float32)
            total = taps[count - 1 : count] * part[LEAD:]
            for i in range(count - 1):
                total += taps[i : i + 1] * pltpu.roll(part, count - 1 - i, 0)[LEAD:]
            out_ref[r * rows : (r + 1) * rows, lanes] = silu(total).astype(jnp.bfloat16)

    if only is not None:
        lanes_step(only)
    elif chunks <= 2:
        for k in range(chunks):
            lanes_step(k)
    else:
        each(chunks, lanes_step)


def kernel(
    blocks, members, rows, per_group, eps,
    x_hbm, b_hbm, c_hbm, z_hbm, dt_hbm, bias_hbm, alog_hbm, skip_hbm, tx_hbm, tb_hbm, tc_hbm, gain_hbm,
    out_ref,
    xbuf, bbuf, cbuf, dtbuf, zbuf, tx, tb, tc, gain, bias, alog, skip,
    xtail, btail, ctail, packed, unpacked, gate,
    xconv, bconv, cconv, rowbuf, colbuf, acc, escale, decay, scaled, enter, leave, outgoing, ret,
    local_sem, send_sem, recv_sem, halo_send, halo_recv, state_send, state_recv, ret_send, ret_recv,
):
    place = lax.axis_index("seq")
    me = lax.rem(place, members)
    block = place // members
    base = block * members
    width = per_group * HEAD_DIM
    pairs = per_group // 2
    high, low = me // 2, lax.rem(me, 2)

    def partner(d):
        return lax.rem(high + d // 2, 2) * 2 + lax.rem(low + d % 2, 2)

    def at(index):
        return {"seq": index}

    has_next = block < blocks - 1
    has_prev = block > 0
    is_last = me == members - 1

    barrier = pltpu.get_barrier_semaphore()
    for d in range(1, members):
        pl.semaphore_signal(barrier, inc=1, device_id=at(base + partner(d)))

    @pl.when(has_prev)
    def _():
        pl.semaphore_signal(barrier, inc=1, device_id=at(base - 1))

    @pl.when(jnp.logical_and(has_prev, jnp.logical_not(is_last)))
    def _():
        pl.semaphore_signal(barrier, inc=1, device_id=at(place - members))

    sources = (dt_hbm, x_hbm, b_hbm, c_hbm)
    buffers = (dtbuf, xbuf, bbuf, cbuf)
    widths = (None, width, STATE, STATE)

    def piece(n, group):
        if widths[n] is None:
            return sources[n]
        return sources[n].at[:, aligned(group, widths[n])]

    def slot(n, member):
        if widths[n] is None:
            return buffers[n].at[member]
        return buffers[n].at[pl.ds(pl.multiple_of(member * rows + LEAD, LEAD), rows)]

    own = [pltpu.make_async_copy(piece(n, me), slot(n, me), local_sem.at[n]) for n in range(4)]
    small = [
        pltpu.make_async_copy(tx_hbm.at[:, aligned(me, width)], tx, local_sem.at[4]),
        pltpu.make_async_copy(tb_hbm.at[:, aligned(me, STATE)], tb, local_sem.at[5]),
        pltpu.make_async_copy(tc_hbm.at[:, aligned(me, STATE)], tc, local_sem.at[6]),
        pltpu.make_async_copy(gain_hbm, gain, local_sem.at[7]),
        pltpu.make_async_copy(z_hbm, zbuf, local_sem.at[8]),
        pltpu.make_async_copy(bias_hbm, bias, local_sem.at[9]),
        pltpu.make_async_copy(alog_hbm, alog, local_sem.at[10]),
        pltpu.make_async_copy(skip_hbm, skip, local_sem.at[11]),
    ]
    tails = [
        pltpu.make_async_copy(hbm.at[rows - LEAD : rows], tail, local_sem.at[12 + k])
        for k, (hbm, tail) in enumerate(((x_hbm, xtail), (b_hbm, btail), (c_hbm, ctail)))
    ]
    sends_halo = jnp.logical_and(has_next, is_last)

    @pl.when(sends_halo)
    def _():
        for copy in tails:
            copy.start()

    for copy in own + small:
        copy.start()

    @pl.when(jnp.logical_not(has_prev))
    def _():
        for buf in (xbuf, bbuf, cbuf):
            buf[0:LEAD] = jnp.zeros((LEAD, buf.shape[1]), jnp.bfloat16)
        enter[...] = jnp.zeros_like(enter)

    next_count = jnp.where(is_last, members, 1)
    pl.semaphore_wait(barrier, members - 1 + jnp.where(has_next, next_count, 0))

    sends = {}
    for n in range(4):
        for d in (3, 2, 1):
            sends[n, d] = pltpu.make_async_remote_copy(
                src_ref=piece(n, partner(d)),
                dst_ref=slot(n, me),
                send_sem=send_sem.at[n, d - 1],
                recv_sem=recv_sem.at[n, d - 1],
                device_id=at(base + partner(d)),
            )

    def halo(member):
        return pltpu.make_async_remote_copy(
            src_ref=packed.at[member],
            dst_ref=unpacked,
            send_sem=halo_send.at[member],
            recv_sem=halo_recv,
            device_id=at(base + members + member),
        )

    def start(n):
        for d in (3, 2, 1):
            sends[n, d].start()

    for n in range(3):
        start(n)

    yields = lax.axis_index("head") > 0

    @pl.when(jnp.logical_not(yields))
    def _():
        start(3)

    spots = halo_spots(width)
    inside = lax.broadcasted_iota(jnp.int32, (LEAD, 128), 0)

    @pl.when(sends_halo)
    def _():
        for copy in tails:
            copy.wait()
        for member in range(members):
            tile = jnp.zeros((LEAD, 128), jnp.float32)
            for q, (n, start) in enumerate(spots):
                place_in = 3 * (q % 5)
                tail = (xtail, btail, ctail)[n]
                offset = member * (width if n == 0 else STATE) + start
                part = tail[:, offset : offset + 128].astype(jnp.float32)
                part = pltpu.roll(part, (place_in + 3) % LEAD, 0)
                fits = jnp.logical_and(inside >= place_in, inside < place_in + 3)
                tile = jnp.where(fits, part, tile)
                if q % 5 == 4 or q == len(spots) - 1:
                    first = q // 5 * LEAD
                    packed[member, first : first + LEAD] = tile.astype(jnp.bfloat16)
            halo(member).start()

    def take_halo():
        @pl.when(has_prev)
        def _():
            halo(0).wait_recv()
            for q, (n, start) in enumerate(spots):
                first = q // 5 * LEAD
                tile = unpacked[first : first + LEAD].astype(jnp.float32)
                part = pltpu.roll(tile, (13 - 3 * (q % 5)) % LEAD, 0)
                buffers[n + 1][0:LEAD, start : start + 128] = part.astype(jnp.bfloat16)

    def arrive(n):
        own[n].wait()
        for d in (1, 2, 3):
            sends[n, d].wait_recv()

    arrive(0)
    raw = jnp.concatenate([dtbuf[m] for m in range(members)], axis=1).astype(jnp.float32)
    for copy in small[5:]:
        copy.wait()
    heads_here = raw.shape[0]
    head_id = lax.broadcasted_iota(jnp.int32, (heads_here, BLOCK), 0)
    sub = lax.broadcasted_iota(jnp.int32, (8, BLOCK), 0)
    up_to = (
        lax.broadcasted_iota(jnp.int32, (BLOCK, BLOCK), 0)
        <= lax.broadcasted_iota(jnp.int32, (BLOCK, BLOCK), 1)
    ).astype(jnp.float32).astype(jnp.bfloat16)

    def rates_step(p):
        first = me * per_group + 2 * p

        def row(k):
            return jnp.sum(jnp.where(head_id == first + k, raw, 0.0), axis=0, keepdims=True)

        def both(ref):
            return jnp.where(sub == 0, ref[first], ref[first + 1])

        v = jnp.where(sub == 0, row(0), row(1)) + both(bias)
        rates = jnp.maximum(v, 0.0) + jnp.log1p(jnp.exp(-jnp.abs(v)))
        decays = rates * -jnp.exp(both(alog))
        top = decays.astype(jnp.bfloat16).astype(jnp.float32)
        rest = decays - top
        middle = rest.astype(jnp.bfloat16).astype(jnp.float32)
        stacked = jnp.concatenate([top, middle, rest - middle, jnp.zeros_like(top)], axis=0)
        summed = jnp.dot(stacked.astype(jnp.bfloat16), up_to, preferred_element_type=jnp.float32)
        log_decay = summed[0:8] + summed[8:16] + summed[16:24]
        weight = jnp.exp(log_decay[:, BLOCK - 1 : BLOCK] - log_decay) * rates
        rowbuf[p, 0:8] = log_decay
        rowbuf[p, 8:16] = rates
        colbuf[p] = jnp.transpose(
            jnp.concatenate([log_decay, weight, jnp.exp(log_decay)], axis=0)
        )

    half = BLOCK // 2
    bands = []
    for r in range(2):
        span, reach = slice(r * half, (r + 1) * half), (r + 1) * half
        causal = lax.broadcasted_iota(jnp.int32, (half, reach), 0) + r * half >= (
            lax.broadcasted_iota(jnp.int32, (half, reach), 1)
        )
        bands.append((span, reach, causal))

    first_half = lax.broadcasted_iota(jnp.int32, (BLOCK, PAIR), 1) < HEAD_DIM

    def spread(p, column):
        return jnp.where(
            first_half, colbuf[p, :, column : column + 1], colbuf[p, :, column + 1 : column + 2]
        )

    def decay_step(p):
        for span, reach, causal in bands:
            for k in range(2):
                gap = colbuf[p, span, k : k + 1] - rowbuf[p, k : k + 1, 0:reach]
                decay[2 * p + k, span, 0:reach] = jnp.where(
                    causal,
                    jnp.exp(jnp.where(causal, gap, 0.0)) * rowbuf[p, 8 + k : 9 + k, 0:reach],
                    0.0,
                )
        escale[:, aligned(p, PAIR)] = spread(p, 16)

    each(pairs, rates_step)
    each(pairs, decay_step)
    for copy in small[3:5]:
        copy.wait()
    for group in range(members):
        lanes = slice(group * width, (group + 1) * width)
        gate[:, lanes] = silu(zbuf[:, lanes].astype(jnp.float32))

    for copy in small[:3]:
        copy.wait()
    take_halo()
    arrive(1)
    conv_into(xconv, xbuf, tx, rows, width)
    def scale_step(p):
        scaled[:, aligned(p, PAIR)] = (
            xconv[:, aligned(p, PAIR)].astype(jnp.float32) * spread(p, 8)
        ).astype(jnp.bfloat16)

    each(pairs, scale_step)
    arrive(2)

    halves = [slice(k * 128, (k + 1) * 128) for k in range(STATE // 128)]
    carries = [
        pltpu.make_async_remote_copy(
            src_ref=leave.at[:, lanes],
            dst_ref=enter.at[:, lanes],
            send_sem=state_send.at[k],
            recv_sem=state_recv.at[k],
            device_id=at(place + members),
        )
        for k, lanes in enumerate(halves)
    ]

    def take_states():
        @pl.when(has_prev)
        def _():
            for carry in carries:
                carry.wait_recv()

    if blocks > 2:
        take_states()

    for k, lanes in enumerate(halves):
        conv_into(bconv, bbuf, tb, rows, STATE, k)

        @pl.when(has_next)
        def _(k=k, lanes=lanes):
            def state_step(p):
                fresh = lax.dot_general(
                    scaled[:, aligned(p, PAIR)], bconv[:, lanes], TN,
                    preferred_element_type=jnp.float32,
                )
                if blocks > 2:
                    total = jnp.exp(rowbuf[p, 0:8, BLOCK - 1 : BLOCK])
                    upper = lax.broadcasted_iota(jnp.int32, (PAIR, 128), 0) < HEAD_DIM
                    fresh += jnp.where(upper, total[0:1], total[1:2]) * enter[aligned(p, PAIR), lanes]
                leave[aligned(p, PAIR), lanes] = fresh.astype(leave.dtype)

            each(pairs, state_step)
            carries[k].start()

    @pl.when(yields)
    def _():
        start(3)

    arrive(3)
    conv_into(cconv, cbuf, tc, rows, STATE)
    scores = [
        lax.dot_general(cconv[span], bconv[0:reach], NT, preferred_element_type=jnp.float32)
        for span, reach, _ in bands
    ]

    def inner_step(p):
        x_pair = xconv[:, aligned(p, PAIR)]
        x_wide = x_pair.astype(jnp.float32)
        first = me * per_group + 2 * p
        direct = jnp.where(first_half, skip[first], skip[first + 1]) * x_wide
        x_mine = [
            jnp.where(mine, x_wide, 0.0).astype(jnp.bfloat16)
            for mine in (first_half, jnp.logical_not(first_half))
        ]
        for score, (span, reach, _) in zip(scores, bands):
            total = direct[span]
            for k in range(2):
                mixing = (score * decay[2 * p + k, span, 0:reach]).astype(jnp.bfloat16)
                total += jnp.dot(mixing, x_mine[k][0:reach], preferred_element_type=jnp.float32)
            acc[span, aligned(p, PAIR)] = total

    each(pairs, inner_step)

    if blocks == 2:
        take_states()

    returns = {
        d: pltpu.make_async_remote_copy(
            src_ref=outgoing.at[d - 1],
            dst_ref=ret.at[me],
            send_sem=ret_send.at[d - 1],
            recv_sem=ret_recv.at[d - 1],
            device_id=at(base + partner(d)),
        )
        for d in (3, 2, 1)
    }

    def finish(with_outer):
        for d in (3, 2, 1, 0):
            here = pl.ds(pl.multiple_of(partner(d) * rows, rows), rows)
            result = acc[here]
            if with_outer:
                result += escale[here] * lax.dot_general(
                    cconv[here], enter[...].astype(jnp.bfloat16), NT,
                    preferred_element_type=jnp.float32,
                )
            if d == 0:
                ret[me] = result.astype(jnp.bfloat16)
            else:
                outgoing[d - 1] = result.astype(jnp.bfloat16)
                returns[d].start()

    @pl.when(has_prev)
    def _():
        finish(True)

    @pl.when(jnp.logical_not(has_prev))
    def _():
        finish(False)

    for d in (0, 1, 2, 3):
        if d > 0:
            returns[d].wait_recv()
        group = partner(d)
        lanes = aligned(group, width)
        gated = ret[group].astype(jnp.float32) * gate[:, lanes]
        mean_square = jnp.sum(gated * gated, axis=-1, keepdims=True) * (1.0 / width)
        out_ref[:, lanes] = (gated * lax.rsqrt(mean_square + eps) * gain[:, lanes]).astype(
            jnp.bfloat16
        )

    for n in range(4):
        for d in (1, 2, 3):
            sends[n, d].wait_send()

    @pl.when(sends_halo)
    def _():
        for member in range(members):
            halo(member).wait_send()

    @pl.when(has_next)
    def _():
        for carry in carries:
            carry.wait_send()

    for d in (1, 2, 3):
        returns[d].wait_send()


def body(x_in, b_in, c_in, z_in, dt_raw, dt_bias, a_log, d_skip, conv_x, conv_b, conv_c, norm_gain):
    rows, channels = x_in.shape
    heads_here = dt_raw.shape[1]
    groups_here = b_in.shape[1] // STATE
    per_group = heads_here // groups_here
    members = BLOCK // rows
    blocks = lax.axis_size("seq") // members
    assert members == 4 and groups_here == members and per_group % 2 == 0
    width = per_group * HEAD_DIM
    pairs = per_group // 2
    tiles = halo_tiles(width)
    taps = conv_x.shape[0]
    carried = jnp.bfloat16 if blocks == 2 else jnp.float32
    low, full = jnp.bfloat16, jnp.float32
    dma = pltpu.SemaphoreType.DMA
    hbm = pl.BlockSpec(memory_space=pltpu.HBM)
    operands = [
        pltpu.with_memory_space_constraint(value, pltpu.HBM)
        for value in (
            x_in, b_in, c_in, z_in, dt_raw.T, dt_bias, a_log, d_skip,
            conv_x, conv_b, conv_c, norm_gain.reshape(1, channels),
        )
    ]
    return pl.pallas_call(
        functools.partial(kernel, blocks, members, rows, per_group, 1e-5),
        out_shape=jax.ShapeDtypeStruct((rows, channels), jnp.bfloat16),
        in_specs=[hbm] * 12,
        out_specs=pl.BlockSpec(memory_space=pltpu.VMEM),
        scratch_shapes=[
            pltpu.VMEM((LEAD + BLOCK, width), low),
            pltpu.VMEM((LEAD + BLOCK, STATE), low),
            pltpu.VMEM((LEAD + BLOCK, STATE), low),
            pltpu.VMEM((members, heads_here, rows), low),
            pltpu.VMEM((rows, channels), low),
            pltpu.VMEM((taps, width), low),
            pltpu.VMEM((taps, STATE), low),
            pltpu.VMEM((taps, STATE), low),
            pltpu.VMEM((1, channels), full),
            pltpu.SMEM((heads_here,), full),
            pltpu.SMEM((heads_here,), full),
            pltpu.SMEM((heads_here,), full),
            pltpu.VMEM((LEAD, channels), low),
            pltpu.VMEM((LEAD, b_in.shape[1]), low),
            pltpu.VMEM((LEAD, b_in.shape[1]), low),
            pltpu.VMEM((members, tiles * LEAD, 128), low),
            pltpu.VMEM((tiles * LEAD, 128), low),
            pltpu.VMEM((rows, channels), full),
            pltpu.VMEM((BLOCK, width), low),
            pltpu.VMEM((BLOCK, STATE), low),
            pltpu.VMEM((BLOCK, STATE), low),
            pltpu.VMEM((pairs, 16, BLOCK), full),
            pltpu.VMEM((pairs, BLOCK, 24), full),
            pltpu.VMEM((BLOCK, width), full),
            pltpu.VMEM((BLOCK, width), full),
            pltpu.VMEM((per_group, BLOCK, BLOCK), full),
            pltpu.VMEM((BLOCK, width), low),
            pltpu.VMEM((width, STATE), carried),
            pltpu.VMEM((width, STATE), carried),
            pltpu.VMEM((members - 1, rows, width), low),
            pltpu.VMEM((members, rows, width), low),
            dma((15,)),
            dma((4, 3)),
            dma((4, 3)),
            dma((members,)),
            dma,
            dma((2,)),
            dma((2,)),
            dma((3,)),
            dma((3,)),
        ],
        compiler_params=pltpu.CompilerParams(
            collective_id=0, has_side_effects=True, vmem_limit_bytes=32 * 1024 * 1024
        ),
    )(
        *operands,
    )


def solution(mesh):
    placed = (
        P(("rep", "seq"), "head"),
        P(("rep", "seq"), "head"),
        P(("rep", "seq"), "head"),
        P(("rep", "seq"), "head"),
        P(("rep", "seq"), "head"),
        P("head"),
        P("head"),
        P("head"),
        P(None, "head"),
        P(None, "head"),
        P(None, "head"),
        P("head"),
    )
    return jax.shard_map(
        body, mesh=mesh, in_specs=placed, out_specs=P(("rep", "seq"), "head"), check_vma=False
    )
```
